32 devices in a mesh: ctx: 8 (over z, y), head: 4 (over x, core).
Axes of the slice: x: 2, y: 2, z: 4, core: 2. Of those that a mesh axis runs over, the one named last changes fastest.
Arguments:
- queries: bfloat16 [1024, 73728], P('ctx', 'head'), may hold values from -6 to 6
- latent: bfloat16 [1024, 576], P('ctx'), may hold values from -6 to 6
- gate: float32 [1024, 128], P('ctx', 'head'), may hold values from -6 to 6
- d_out: bfloat16 [1024, 65536], P('ctx', 'head'), may hold values from -6 to 6
- segments: int32 [1024], replicated, may hold values from 0 to 15, never falling along the last dimension, each value on 1 to 128 neighbouring positions
Outputs:
- d_queries: bfloat16 [1024, 73728], P('ctx', 'head')
- d_gate: float32 [1024, 128], P('ctx', 'head')
- d_latent: float32 [1024, 576], P('ctx')
The draws below stay inside these ranges and needn't reach their ends.
Inputs may be any that keep to these rules, and one draw needn't show every extreme that they name: `segments`: ids never fall along the tokens; every document has 1 to 128 tokens, so it covers at most two neighbouring ctx shards.
All inputs are finite; a program needn't handle non-finite values.
Results may differ from the reference program's by a relative error of at most 0.013.
Values may be sent and summed in bfloat16 or wider, within the bound.
No kernel may reach another device: no remote copies, remote signals or barrier semaphores. Data moves between devices by JAX's collectives and lax.ppermute only.
A program may use at most 64 MiB of HBM per device.

```python
import math
import jax
import jax.numpy as jnp
import numpy as np
from jax import lax

HEADS = 128
LATENT = 512
ROPE = 64
TOK_DEV = 128
TOKENS = 1024
DOCS = 16


def levels(stream_key, extent, shards, least, largest):
    def one(dim, shards_of):
        heights = jax.random.uniform(jax.random.fold_in(jax.random.fold_in(stream_key, 6), dim), (shards_of,), jnp.float32, least / len(shards), largest / len(shards))
        return jnp.repeat(jnp.exp(heights), extent[dim] // shards_of).reshape((-1,) + (1,) * (len(extent) - dim - 1))

    gain = one(*shards[0])
    for cut in shards[1:]:
        gain = gain * one(*cut)
    return gain


def length_profile(number_of, total, most, slope):
    weights = [(1 << 20) // math.isqrt(grade ** slope) + 1 for grade in range(2, number_of + 1)]
    surplus, given = total - most - (number_of - 1), [1] * (number_of - 1)
    while surplus > 0:
        candidates = [i for i in range(number_of - 1) if given[i] < most]
        whole, remaining = sum([weights[i] for i in candidates]), surplus
        for i in candidates:
            addition = min(most - given[i], max(1, remaining * weights[i] // whole), surplus)
            given[i] = given[i] + addition
            surplus = surplus - addition
    return np.array([most] + given)


def ragged(rng, amount, total, most, lean):
    if amount == 2:
        one = jax.random.randint(rng, (), max(1, total - most), min(most, total - 1) + 1)
        return jnp.stack([one, total - one])
    tallies = jnp.asarray(length_profile(amount, total, most, lean), jnp.int32)
    pairs = (amount - 1) // 2
    donor, taker = tallies[1:1 + 2 * pairs:2], tallies[2:2 + 2 * pairs:2]
    slack = jnp.minimum(donor - 1, most - taker)
    passed = jax.random.randint(jax.random.fold_in(rng, 1), (pairs,), 0, 1 << 20) % (slack + 1)
    tallies = tallies.at[1:1 + 2 * pairs:2].set(donor - passed).at[2:2 + 2 * pairs:2].set(taker + passed)
    return tallies[jax.random.permutation(jax.random.fold_in(rng, 2), amount)]


def scatter_about(stream_key, dims, spread, limit, split=(), held_as=jnp.bfloat16):
    values = jax.random.normal(stream_key, dims, jnp.float32) * spread
    if len(split) > 0:
        values = levels(stream_key, dims, split, -0.22, 0.18) * values
    return jnp.clip(values, min=-limit, max=limit).astype(held_as)


def setup_inputs(seed: int = 0) -> dict:
    key_list = jax.random.split(jax.random.key(seed), 6)
    return {
        "queries": scatter_about(key_list[0], (TOKENS, HEADS * (LATENT + ROPE)), 1.0, 6.0, ((0, 8), (1, 4))),
        "latent": scatter_about(key_list[1], (TOKENS, LATENT + ROPE), 1.0, 6.0, ((0, 8),)),
        "gate": scatter_about(key_list[2], (TOKENS, HEADS), 1.5, 6.0, ((0, 8), (1, 4)), jnp.float32),
        "d_out": scatter_about(key_list[3], (TOKENS, HEADS * LATENT), 1.0, 6.0, ((0, 8), (1, 4))),
        "segments": jnp.searchsorted(jnp.cumsum(ragged(key_list[4], DOCS, TOKENS, TOK_DEV, 2)), jnp.arange(TOKENS), side="right").astype(jnp.int32),
    }


SCALE = 192.0 ** -0.5
CAP = 20.0


def build_allowed(segments, shard_index, tok_rows):
    first_row = shard_index * tok_rows
    query_seg = lax.dynamic_slice_in_dim(segments, first_row, tok_rows)
    prior_seg = lax.dynamic_slice_in_dim(segments, jnp.maximum(first_row - tok_rows, 0).astype(jnp.int32), tok_rows)
    key_seg = jnp.concatenate([prior_seg, query_seg])
    query_pos = first_row + jnp.arange(tok_rows, dtype=jnp.int32)
    key_pos = first_row - tok_rows + jnp.arange(2 * tok_rows, dtype=jnp.int32)
    same_doc = key_seg[None, :] == query_seg[:, None]
    return same_doc & (key_pos[None, :] <= query_pos[:, None]) & (key_pos[None, :] >= 0)


def local_grads(query_blk, all_keys, gate_blk, cotangent, allowed):
    f32 = jnp.float32
    values = all_keys[:, :LATENT]
    raw = jnp.einsum("qhd,kd->hqk", query_blk.astype(f32), all_keys.astype(f32)) * SCALE
    squashed = jnp.tanh(raw / CAP)
    weights = jnp.where(allowed[None], jnp.exp(CAP * squashed), 0.0)
    probs = weights / jnp.sum(weights, axis=2, keepdims=True)
    probs_low = probs.astype(jnp.bfloat16)
    attended = jnp.einsum("hqk,kd->qhd", probs_low.astype(f32), values.astype(f32))
    opened = jax.nn.sigmoid(gate_blk)
    gate_grad = opened * (1.0 - opened) * jnp.sum(cotangent.astype(f32) * attended, axis=2)
    d_att = (opened[:, :, None] * cotangent.astype(f32)).astype(jnp.bfloat16)
    row_dot = jnp.sum(d_att.astype(f32) * attended, axis=2)
    d_probs = jnp.einsum("qhd,kd->hqk", d_att.astype(f32), values.astype(f32))
    d_raw = (probs * (d_probs - row_dot.T[:, :, None]) * (1.0 - squashed * squashed) * SCALE).astype(jnp.bfloat16)
    d_query = jnp.einsum("hqk,kd->qhd", d_raw.astype(f32), all_keys.astype(f32))
    d_keys = jnp.einsum("hqk,qhd->kd", d_raw.astype(f32), query_blk.astype(f32))
    d_values = jnp.einsum("hqk,qhd->kd", probs_low.astype(f32), d_att.astype(f32))
    d_total = d_keys + jnp.pad(d_values, ((0, 0), (0, ROPE)))
    return d_query, gate_grad, d_total


def reference(queries, latent, gate, d_out, segments):
    tok_rows = TOK_DEV
    shard_count = TOKENS // TOK_DEV
    width = LATENT + ROPE
    query_all = queries.reshape(shard_count, tok_rows, HEADS, width)
    latent_all = latent.reshape(shard_count, tok_rows, width)
    prior_all = jnp.concatenate([jnp.zeros_like(latent_all[:1]), latent_all[:-1]], axis=0)
    gate_all = gate.reshape(shard_count, tok_rows, HEADS)
    cot_all = d_out.reshape(shard_count, tok_rows, HEADS, LATENT)

    def per_shard(blocks):
        shard_index, query_blk, prior_blk, latent_blk, gate_blk, cot_blk = blocks
        all_keys = jnp.concatenate([prior_blk, latent_blk], axis=0)
        allowed = build_allowed(segments, shard_index, tok_rows)
        return local_grads(query_blk, all_keys, gate_blk, cot_blk, allowed)

    shard_ids = jnp.arange(shard_count, dtype=jnp.int32)
    d_query, gate_grad, d_total = lax.map(per_shard, (shard_ids, query_all, prior_all, latent_all, gate_all, cot_all))
    owned = d_total[:, tok_rows:]
    earlier = d_total[:, :tok_rows]
    returned = jnp.concatenate([earlier[1:], jnp.zeros_like(earlier[:1])], axis=0)
    d_latent = (owned + returned).reshape(TOKENS, width)
    d_queries = d_query.reshape(TOKENS, HEADS * width).astype(jnp.bfloat16)
    return d_queries, gate_grad.reshape(TOKENS, HEADS), d_latent
```

```python
import functools

import jax
import jax.numpy as jnp
from jax import lax
from jax.experimental import pallas as pl
from jax.experimental.pallas import tpu as pltpu
from jax.sharding import PartitionSpec as P

LATENT = 512
ROPE = 64
WIDTH = LATENT + ROPE
PAIR = 2 * WIDTH
PADDED = LATENT + 2 * ROPE
SCALE = 192.0 ** (-0.5)
CAP = 20.0
BF16 = jnp.bfloat16
F32 = jnp.float32


def dot_tt(a, b):
    return lax.dot_general(a, b, (((1,), (1,)), ((), ())), preferred_element_type=F32)


def dot_nn(a, b):
    return lax.dot_general(a, b, (((1,), (0,)), ((), ())), preferred_element_type=F32)


def padded_keys(keys_t):
    spare = jnp.zeros((ROPE, keys_t.shape[1]), keys_t.dtype)
    even = jnp.concatenate([keys_t, spare], axis=0).T
    odd = jnp.concatenate([spare, keys_t], axis=0).T
    return even, odd


def latent_grad_t(even, odd, values):
    first = even + jnp.concatenate([values, jnp.zeros((values.shape[0], 2 * ROPE), F32)], axis=1)
    return first.T[:WIDTH] + odd.T[ROPE:]


def head_slots(quad):
    return (4 * quad, 4 * quad + 2, 4 * quad + 1, 4 * quad + 3)


def own_scores(q_hbm, g_hbm, keys_t, scores, d_probs, q_all, g_all, sems):
    tok = keys_t.shape[1]
    quads = q_all.shape[0] // (2 * tok)
    copies = []
    for quad in range(quads):
        group = []
        for pair in (2 * quad, 2 * quad + 1):
            group.append((q_hbm.at[:, pl.ds(pair * PAIR, PAIR)], q_all.at[pl.ds(pair * tok, tok), :]))
        for slot, head in enumerate(head_slots(quad)):
            group.append(
                (g_hbm.at[:, pl.ds(head * LATENT, LATENT)], g_all.at[pl.ds((4 * quad + slot) * tok, tok), :])
            )
        copies.append([pltpu.make_async_copy(s, d, sems.at[quad, n]) for n, (s, d) in enumerate(group)])
        for copy in copies[-1]:
            copy.start()
    even, odd = padded_keys(keys_t[...])
    for quad in range(quads):
        for copy in copies[quad]:
            copy.wait()
        rows = pl.ds(quad * 2 * tok, 2 * tok)
        base = quad * 4 * tok
        scores[:, pl.ds(base, 2 * tok)] = dot_tt(even, q_all[rows, pl.ds(0, PADDED)])
        scores[:, pl.ds(base + 2 * tok, 2 * tok)] = dot_tt(odd, q_all[rows, pl.ds(LATENT, PADDED)])
        d_probs[:, pl.ds(base, 4 * tok)] = dot_tt(even[:, :LATENT], g_all[pl.ds(base, 4 * tok), :])


def prior_part(
    index, own_s, own_d, q_all, g_all, prior_t, gate_t, segments,
    d_raw, d_val, d_gate, early_t, acc_even, acc_odd, acc_val,
):
    tok = prior_t.shape[1]
    quads = q_all.shape[0] // (2 * tok)
    shard = index[0]
    even, odd = padded_keys(prior_t[...])
    row_own = segments[pl.ds(shard, 1), :]
    row_prior = segments[pl.ds(jnp.maximum(shard - 1, 0), 1), :]
    key_own = jnp.broadcast_to(row_own, (tok, tok)).T
    key_prior = jnp.broadcast_to(row_prior, (tok, tok)).T
    key_at = lax.broadcasted_iota(jnp.int32, (tok, tok), 0)
    query_at = lax.broadcasted_iota(jnp.int32, (tok, tok), 1)
    early = key_at > query_at
    same = jnp.where(early, key_prior, key_own) == row_own
    allowed = same & (jnp.logical_not(early) | (shard > 0))
    early = jnp.concatenate([early, early], axis=1)
    allowed = jnp.concatenate([allowed, allowed], axis=1)
    acc_even[...] = jnp.zeros_like(acc_even)
    acc_odd[...] = jnp.zeros_like(acc_odd)
    acc_val[...] = jnp.zeros_like(acc_val)

    def half(cols, heads, keys, q_blk, g_blk):
        raw = jnp.where(early, dot_tt(keys, q_blk), own_s[:, cols])
        d_p = jnp.where(early, dot_tt(even[:, :LATENT], g_blk), own_d[:, cols])
        squashed = jnp.tanh(raw * (SCALE / CAP))
        weights = jnp.where(allowed, jnp.exp(CAP * squashed), 0.0)
        total = jnp.sum(weights, axis=0, keepdims=True)
        opened = jax.nn.sigmoid(jnp.concatenate([gate_t[pl.ds(h, 1), :] for h in heads], axis=1))
        inverse = 1.0 / total
        mean = jnp.sum(weights * d_p, axis=0, keepdims=True) * inverse
        gate_grad = opened * (1.0 - opened) * mean
        for n, h in enumerate(heads):
            d_gate[pl.ds(h, 1), :] = gate_grad[:, n * tok : (n + 1) * tok]
        gated = weights * (inverse * opened)
        slope = gated * (d_p - mean) * (SCALE - SCALE * squashed * squashed)
        gated, slope = gated.astype(BF16), slope.astype(BF16)
        d_raw[:, cols] = slope
        d_val[:, cols] = gated
        zero = jnp.zeros_like(slope)
        return jnp.where(early, slope, zero), jnp.where(early, gated, zero)

    for quad in range(quads):
        rows = pl.ds(quad * 2 * tok, 2 * tok)
        base = quad * 4 * tok
        heads = head_slots(quad)
        for odd_half, keys, acc, at in ((0, even, acc_even, 0), (1, odd, acc_odd, LATENT)):
            cols = pl.ds(base + odd_half * 2 * tok, 2 * tok)
            q_blk = q_all[rows, pl.ds(at, PADDED)]
            g_blk = g_all[cols, :]
            slope, gated = half(cols, heads[2 * odd_half : 2 * odd_half + 2], keys, q_blk, g_blk)
            acc[...] += dot_nn(slope, q_blk)
            acc_val[...] += dot_nn(gated, g_blk)
    early_t[...] = latent_grad_t(acc_even[...], acc_odd[...], acc_val[...]).astype(early_t.dtype)


def own_part(d_raw, d_val, q_all, g_all, own_t, acc_even, acc_odd, acc_val):
    tok = d_raw.shape[0]
    quads = q_all.shape[0] // (2 * tok)
    key_at = lax.broadcasted_iota(jnp.int32, (tok, 2 * tok), 0)
    query_at = lax.broadcasted_iota(jnp.int32, (tok, 2 * tok), 1) % tok
    early = key_at > query_at
    acc_even[...] = jnp.zeros_like(acc_even)
    acc_odd[...] = jnp.zeros_like(acc_odd)
    acc_val[...] = jnp.zeros_like(acc_val)
    zero = jnp.zeros((tok, 2 * tok), BF16)
    for quad in range(quads):
        rows = pl.ds(quad * 2 * tok, 2 * tok)
        for odd_half, acc, at in ((0, acc_even, 0), (1, acc_odd, LATENT)):
            cols = pl.ds(quad * 4 * tok + odd_half * 2 * tok, 2 * tok)
            acc[...] += dot_nn(jnp.where(early, zero, d_raw[:, cols]), q_all[rows, pl.ds(at, PADDED)])
            acc_val[...] += dot_nn(jnp.where(early, zero, d_val[:, cols]), g_all[cols, :])
    own_t[...] = latent_grad_t(acc_even[...], acc_odd[...], acc_val[...])


def query_grads(d_raw, prior_t, keys_t, out_hbm, stage, sems):
    tok = d_raw.shape[0]
    quads = d_raw.shape[1] // (4 * tok)
    even_prior, odd_prior = padded_keys(prior_t[...])
    even_own, odd_own = padded_keys(keys_t[...])
    even = jnp.concatenate([even_prior, even_own], axis=0)
    odd = jnp.concatenate([odd_prior, odd_own], axis=0)
    middle = jnp.concatenate([even[:, LATENT:], odd[:, : 2 * ROPE]], axis=0)
    query_at = lax.broadcasted_iota(jnp.int32, (2 * tok, tok), 0) % tok
    key_at = lax.broadcasted_iota(jnp.int32, (2 * tok, tok), 1)
    early = key_at > query_at
    zero = jnp.zeros((2 * tok, tok), BF16)

    def unfolded(cols):
        slope = d_raw[:, cols].T
        return jnp.concatenate([jnp.where(early, slope, zero), jnp.where(early, zero, slope)], axis=1)

    def copies(quad):
        slot = quad % 2
        return [
            pltpu.make_async_copy(
                stage.at[slot, pl.ds(n * tok, tok), :],
                out_hbm.at[:, pl.ds((2 * quad + n) * PAIR, PAIR)],
                sems.at[slot, n],
            )
            for n in range(2)
        ]

    for quad in range(quads):
        if quad >= 2:
            for copy in copies(quad - 2):
                copy.wait()
        slot = quad % 2
        first = unfolded(pl.ds(quad * 4 * tok, 2 * tok))
        second = unfolded(pl.ds(quad * 4 * tok + 2 * tok, 2 * tok))
        stage[slot, :, pl.ds(0, LATENT)] = dot_nn(first, even[:, :LATENT]).astype(BF16)
        stage[slot, :, pl.ds(LATENT, 2 * ROPE)] = dot_nn(
            jnp.concatenate([first, second], axis=1), middle
        ).astype(BF16)
        stage[slot, :, pl.ds(LATENT + 2 * ROPE, LATENT)] = dot_nn(second, odd[:, 2 * ROPE :]).astype(BF16)
        for copy in copies(quad):
            copy.start()
    for quad in range(max(0, quads - 2), quads):
        for copy in copies(quad):
            copy.wait()


def shifted(value, axis, steps):
    count = lax.axis_size(axis)
    first, last = (max(0, -steps), min(count, count - steps))
    return lax.ppermute(value, axis, [(source, source + steps) for source in range(first, last)])


def shards(queries, latent, gate, d_out, segments):
    tok = latent.shape[0]
    heads = gate.shape[1]
    columns = heads * tok
    vmem = pl.BlockSpec(memory_space=pltpu.VMEM)
    smem = pl.BlockSpec(memory_space=pltpu.SMEM)
    hbm = pl.BlockSpec(memory_space=pl.ANY)
    params = pltpu.CompilerParams(vmem_limit_bytes=24 * 1024 * 1024)
    kept = pltpu.VMEM
    keys_t = latent.T
    gate_t = gate.T
    ids = segments.reshape(-1, tok)
    index = lax.axis_index("ctx").astype(jnp.int32).reshape(1)
    accumulators = [pltpu.VMEM((tok, PADDED), F32), pltpu.VMEM((tok, PADDED), F32), pltpu.VMEM((tok, LATENT), F32)]

    def cost(multiply_adds, moved):
        return pl.CostEstimate(flops=2 * multiply_adds, bytes_accessed=moved, transcendentals=0)

    prior_t = shifted(keys_t, "ctx", 1)
    own_s, own_d, q_all, g_all = pl.pallas_call(
        own_scores,
        out_shape=[
            kept((tok, columns), F32),
            kept((tok, columns), F32),
            kept((columns // 2, PAIR), BF16),
            kept((columns, LATENT), BF16),
        ],
        in_specs=[hbm, hbm, vmem],
        out_specs=[vmem] * 4,
        scratch_shapes=[pltpu.SemaphoreType.DMA((heads // 4, 6))],
        compiler_params=params,
        cost_estimate=cost(columns * tok * (PADDED + LATENT), queries.size * 2 + d_out.size * 2),
        name="own_scores",
    )(queries, d_out, keys_t)
    d_raw, d_val, d_gate_t, early_t = pl.pallas_call(
        prior_part,
        out_shape=[
            kept((tok, columns), BF16),
            kept((tok, columns), BF16),
            jax.ShapeDtypeStruct((heads, tok), F32),
            kept((WIDTH, tok), BF16),
        ],
        in_specs=[smem] + [vmem] * 7,
        out_specs=[vmem] * 4,
        scratch_shapes=accumulators,
        compiler_params=params,
        cost_estimate=cost(2 * columns * tok * (PADDED + LATENT), 0),
        name="prior_part",
    )(index, own_s, own_d, q_all, g_all, prior_t, gate_t, ids)
    returned = shifted(early_t, "ctx", -1)
    own_t = pl.pallas_call(
        own_part,
        out_shape=kept((WIDTH, tok), F32),
        in_specs=[vmem] * 4,
        out_specs=vmem,
        scratch_shapes=accumulators,
        compiler_params=params,
        cost_estimate=cost(columns * tok * (PADDED + LATENT), 0),
        name="own_part",
    )(d_raw, d_val, q_all, g_all)
    d_queries = pl.pallas_call(
        query_grads,
        out_shape=jax.ShapeDtypeStruct(queries.shape, queries.dtype),
        in_specs=[vmem] * 3,
        out_specs=hbm,
        scratch_shapes=[pltpu.VMEM((2, 2 * tok, PAIR), BF16), pltpu.SemaphoreType.DMA((2, 2))],
        compiler_params=params,
        cost_estimate=cost(columns * 2 * tok * PADDED, queries.size * 2),
        name="query_grads",
    )(d_raw, prior_t, keys_t)
    total = own_t + returned.astype(F32)
    group = lax.axis_size("head")
    step = 1
    while step < group:
        sent = total.astype(BF16)
        other = lax.ppermute(sent, "head", [(i, i ^ step) for i in range(group)])
        total = sent.astype(F32) + other.astype(F32)
        step *= 2
    return d_queries, d_gate_t.T, total.T


def solution(mesh):
    placed = (P("ctx", "head"), P("ctx", None), P("ctx", "head"), P("ctx", "head"), P())
    return jax.shard_map(
        shards,
        mesh=mesh,
        in_specs=placed,
        out_specs=(P("ctx", "head"), P("ctx", "head"), P("ctx", None)),
        check_vma=False,
    )
```

```python
import functools

import jax
import jax.numpy as jnp
from jax import lax
from jax.experimental import pallas as pl
from jax.experimental.pallas import tpu as pltpu
from jax.sharding import PartitionSpec as P

LATENT = 512
ROPE = 64
WIDTH = LATENT + ROPE
PAIR = 2 * WIDTH
PADDED = LATENT + 2 * ROPE
SCALE = 192.0 ** (-0.5)
CAP = 20.0
LATE = 3
LOG2_E = 1.4426950408889634
BF16 = jnp.bfloat16
F32 = jnp.float32


def dot_nn(a, b):
    return lax.dot_general(a, b, (((1,), (0,)), ((), ())), preferred_element_type=F32)


def padded_keys(keys_t):
    spare = jnp.zeros((ROPE, keys_t.shape[1]), keys_t.dtype)
    even = jnp.concatenate([keys_t, spare], axis=0).T
    odd = jnp.concatenate([spare, keys_t], axis=0).T
    return even, odd


AHEAD = 3


def head_slots(quad):
    return (4 * quad, 4 * quad + 2, 4 * quad + 1, 4 * quad + 3)


def turn(q_rows, g_rows, q_turned, g_turned, start, tok):
    for n in range(2):
        turned = q_rows[n * tok : (n + 1) * tok].T
        q_turned[:, pl.ds(start + n * tok, tok)] = turned[:WIDTH]
        q_turned[:, pl.ds(start + (2 + n) * tok, tok)] = turned[WIDTH:]
    for n in range(4):
        g_turned[:, pl.ds(start + n * tok, tok)] = g_rows[n * tok : (n + 1) * tok].T


def own_scores(
    q_hbm, g_hbm, keys_hbm,
    scores, d_probs, q_turned, g_turned, q_late, g_late, keys_t,
    q_early, g_early, sems, key_sem,
):
    tok = keys_t.shape[1]
    early, late = q_early.shape[0] // (2 * tok), q_late.shape[0] // (2 * tok)
    quads = early + late
    keys_copy = pltpu.make_async_copy(keys_hbm, keys_t, key_sem.at[0])
    keys_copy.start()

    def copies(quad):
        q_to, g_to, at = (q_early, g_early, quad) if quad < early else (q_late, g_late, quad - early)
        group = []
        for n in range(2):
            group.append(
                (q_hbm.at[:, pl.ds((2 * quad + n) * PAIR, PAIR)], q_to.at[pl.ds((2 * at + n) * tok, tok), :])
            )
        for slot, head in enumerate(head_slots(quad)):
            group.append((g_hbm.at[:, pl.ds(head * LATENT, LATENT)], g_to.at[pl.ds((4 * at + slot) * tok, tok), :]))
        return [pltpu.make_async_copy(s, d, sems.at[quad, n]) for n, (s, d) in enumerate(group)]

    def score(quad):
        for n in range(2):
            cols = pl.ds((4 * quad + 2 * n) * tok, 2 * tok)
            scores[:, cols] = dot_nn(keys, q_turned[:, cols])
            d_probs[:, cols] = dot_nn(keys[:, :LATENT], g_turned[:, cols])

    for quad in range(min(AHEAD, quads)):
        for copy in copies(quad):
            copy.start()
    keys_copy.wait()
    keys = keys_t[...].T
    for quad in range(early):
        if quad + AHEAD < quads:
            for copy in copies(quad + AHEAD):
                copy.start()
        for copy in copies(quad):
            copy.wait()
        turn(
            q_early[pl.ds(2 * quad * tok, 2 * tok), :], g_early[pl.ds(4 * quad * tok, 4 * tok), :],
            q_turned, g_turned, 4 * quad * tok, tok,
        )
        if quad > 0:
            score(quad - 1)
    for quad in range(early + AHEAD, quads):
        for copy in copies(quad):
            copy.start()
    score(early - 1)
    for quad in range(early, quads):
        for copy in copies(quad):
            copy.wait()


def grads(
    own_s, own_d, q_turned, g_turned, q_late, g_late, prior_t, keys_t, gate_t, segments,
    d_raw, d_gate, early_keep, own_keep, send, q_turned_late, g_turned_late, d_val, total,
):
    tok = prior_t.shape[1]
    early_quads, late_quads = q_turned.shape[1] // (4 * tok), q_late.shape[0] // (2 * tok)
    shard = lax.axis_index("ctx")
    prior_keys = prior_t[...].T
    all_keys = jnp.concatenate([prior_keys, keys_t[...].T], axis=0)
    row_own = segments[pl.ds(shard, 1), :]
    row_prior = segments[pl.ds(jnp.maximum(shard - 1, 0), 1), :]
    key_own = jnp.broadcast_to(row_own, (tok, tok)).T
    key_prior = jnp.broadcast_to(row_prior, (tok, tok)).T
    key_at = lax.broadcasted_iota(jnp.int32, (tok, tok), 0)
    query_at = lax.broadcasted_iota(jnp.int32, (tok, tok), 1)
    early = key_at > query_at
    same = jnp.where(early, key_prior, key_own) == row_own
    allowed = same & (jnp.logical_not(early) | (shard > 0))
    early = jnp.concatenate([early, early], axis=1)
    allowed = jnp.concatenate([allowed, allowed], axis=1)
    query_row = lax.broadcasted_iota(jnp.int32, (2 * tok, tok), 0) % tok
    key_column = lax.broadcasted_iota(jnp.int32, (2 * tok, tok), 1)
    early_row = key_column > query_row
    nothing = jnp.zeros((2 * tok, tok), BF16)
    total[...] = jnp.zeros_like(total)

    def place(n):
        quad, odd = n // 2, n % 2
        if quad < early_quads:
            return q_turned, g_turned, pl.ds(n * 2 * tok, 2 * tok)
        return q_turned_late, g_turned_late, pl.ds((n - 2 * early_quads) * 2 * tok, 2 * tok)

    def scores_of(n):
        q_from, g_from, cols = place(n)
        if n < 2 * early_quads:
            raw = dot_nn(prior_keys, q_from[:, cols])
            d_p = dot_nn(prior_keys[:, :LATENT], g_from[:, cols])
            return jnp.where(early, raw, own_s[:, cols]), jnp.where(early, d_p, own_d[:, cols])
        raw = dot_nn(all_keys, q_from[:, cols])
        d_p = dot_nn(all_keys[:, :LATENT], g_from[:, cols])
        return jnp.where(early, raw[:tok], raw[tok:]), jnp.where(early, d_p[:tok], d_p[tok:])

    def softmax_of(n, raw, d_p):
        heads = head_slots(n // 2)[2 * (n % 2) : 2 * (n % 2) + 2]
        squashed = jnp.tanh(raw * (SCALE / CAP))
        weights = jnp.where(allowed, jnp.exp2((CAP * LOG2_E) * squashed), 0.0)
        opened = jax.nn.sigmoid(jnp.concatenate([gate_t[pl.ds(h, 1), :] for h in heads], axis=1))
        inverse = 1.0 / jnp.sum(weights, axis=0, keepdims=True)
        mean = jnp.sum(weights * d_p, axis=0, keepdims=True) * inverse
        gate_grad = opened * (1.0 - opened) * mean
        for at, h in enumerate(heads):
            d_gate[pl.ds(h, 1), :] = gate_grad[:, at * tok : (at + 1) * tok]
        gated = weights * (inverse * opened)
        slope = gated * (d_p - mean) * (SCALE - SCALE * squashed * squashed)
        rows = pl.ds(n * 2 * tok, 2 * tok)
        d_raw[rows, :] = slope.astype(BF16).T
        d_val[rows, :] = gated.astype(BF16).T

    def unfolded(folded):
        return jnp.concatenate(
            [jnp.where(early_row, folded, nothing), jnp.where(early_row, nothing, folded)], axis=1
        )

    def add_up(n):
        q_from, g_from, cols = place(n)
        rows = pl.ds(n * 2 * tok, 2 * tok)
        slope = unfolded(d_raw[rows, :])
        both = jnp.concatenate([slope, unfolded(d_val[rows, :])], axis=0)
        left = jnp.concatenate([q_from[pl.ds(0, LATENT), cols], g_from[:, cols]], axis=1)
        total[pl.ds(0, LATENT), :] += dot_nn(left, both)
        total[pl.ds(LATENT, ROPE), :] += dot_nn(q_from[pl.ds(LATENT, ROPE), cols], slope)

    count = 2 * (early_quads + late_quads)
    raws = {}
    for n in range(count + 2):
        if n % 2 == 0 and n // 2 < late_quads:
            quad = n // 2
            turn(
                q_late[pl.ds(2 * quad * tok, 2 * tok), :], g_late[pl.ds(4 * quad * tok, 4 * tok), :],
                q_turned_late, g_turned_late, 4 * quad * tok, tok,
            )
        if n < count:
            raws[n] = scores_of(n)
        if 1 <= n <= count:
            softmax_of(n - 1, *raws.pop(n - 1))
        if n >= 2:
            add_up(n - 2)
    core = lax.axis_index("head") % 2
    half = WIDTH // 2
    mine = pl.ds(pl.multiple_of(core * half, 32), half)
    others = pl.ds(pl.multiple_of((1 - core) * half, 32), half)
    early_keep[...] = total[mine, :tok]
    own_keep[...] = total[mine, tok:]
    send[...] = total[others, :].astype(send.dtype)


def query_grads(first_quad, d_raw, prior_t, keys_t, after, *refs):
    out_hbm, done, stage, sems = refs[-4:]
    tok = d_raw.shape[1]
    quads = stage.shape[0] // (2 * tok)
    even_prior, odd_prior = padded_keys(prior_t[...])
    even_own, odd_own = padded_keys(keys_t[...])
    even = jnp.concatenate([even_prior, even_own], axis=0)
    odd = jnp.concatenate([odd_prior, odd_own], axis=0)
    middle = jnp.concatenate([even[:, LATENT:], odd[:, : 2 * ROPE]], axis=0)
    query_at = lax.broadcasted_iota(jnp.int32, (2 * tok, tok), 0) % tok
    key_at = lax.broadcasted_iota(jnp.int32, (2 * tok, tok), 1)
    early = key_at > query_at
    zero = jnp.zeros((2 * tok, tok), BF16)

    def unfolded(start):
        slope = d_raw[pl.ds(start, 2 * tok), :]
        return jnp.concatenate([jnp.where(early, slope, zero), jnp.where(early, zero, slope)], axis=1)

    copies = []
    for quad in range(quads):
        base = (first_quad + quad) * 4 * tok
        rows = pl.ds(quad * 2 * tok, 2 * tok)
        first = unfolded(base)
        second = unfolded(base + 2 * tok)
        stage[rows, pl.ds(0, LATENT)] = dot_nn(first, even[:, :LATENT]).astype(BF16)
        stage[rows, pl.ds(LATENT, 2 * ROPE)] = dot_nn(jnp.concatenate([first, second], axis=1), middle).astype(BF16)
        stage[rows, pl.ds(LATENT + 2 * ROPE, LATENT)] = dot_nn(second, odd[:, 2 * ROPE :]).astype(BF16)
        for n in range(2):
            pair = 2 * quad + n
            copies.append(
                pltpu.make_async_copy(
                    stage.at[pl.ds(pair * tok, tok), :],
                    out_hbm.at[:, pl.ds((2 * first_quad + pair) * PAIR, PAIR)],
                    sems.at[pair],
                )
            )
            copies[-1].start()
    for copy in copies:
        copy.wait()


def add_early(keep, other, out):
    out[...] = (keep[...] + other[:, : out.shape[1]].astype(F32)).astype(out.dtype)


def add_own(keep, other, returned, after, out):
    out[...] = (keep[...] + other[:, out.shape[1] :].astype(F32) + returned[...].astype(F32)).astype(out.dtype)


def add_halves(a, b, after, out):
    out[...] = (a[...].astype(F32) + b[...].astype(F32)).astype(out.dtype)


def shifted(value, axis, steps):
    count = lax.axis_size(axis)
    first, last = (max(0, -steps), min(count, count - steps))
    return lax.ppermute(value, axis, [(source, source + steps) for source in range(first, last)])


def shards(queries, latent, gate, d_out, segments):
    tok = latent.shape[0]
    heads = gate.shape[1]
    columns = heads * tok
    vmem = pl.BlockSpec(memory_space=pltpu.VMEM)
    hbm = pl.BlockSpec(memory_space=pl.ANY)
    params = pltpu.CompilerParams(vmem_limit_bytes=28 * 1024 * 1024)
    kept = pltpu.VMEM
    keys_t = latent.T
    gate_t = gate.T
    ids = segments.reshape(-1, tok)
    quads = heads // 4
    late = max(1, (quads * LATE) // 8)
    early = quads - late
    half = WIDTH // 2

    def cost(multiply_adds, moved):
        return pl.CostEstimate(flops=2 * multiply_adds, bytes_accessed=moved, transcendentals=0)

    prior_t = shifted(keys_t, "ctx", 1)
    kernel_in = [pltpu.with_memory_space_constraint(x, pltpu.HBM) for x in (queries, d_out, keys_t)]
    own_s, own_d, q_turned, g_turned, q_late, g_late, keys_t = pl.pallas_call(
        own_scores,
        out_shape=[
            kept((tok, 4 * early * tok), F32),
            kept((tok, 4 * early * tok), F32),
            kept((WIDTH, 4 * early * tok), BF16),
            kept((LATENT, 4 * early * tok), BF16),
            kept((2 * late * tok, PAIR), BF16),
            kept((4 * late * tok, LATENT), BF16),
            kept((WIDTH, tok), BF16),
        ],
        in_specs=[hbm] * 3,
        out_specs=[vmem] * 7,
        scratch_shapes=[
            pltpu.VMEM((2 * early * tok, PAIR), BF16),
            pltpu.VMEM((4 * early * tok, LATENT), BF16),
            pltpu.SemaphoreType.DMA((quads, 6)),
            pltpu.SemaphoreType.DMA((1,)),
        ],
        compiler_params=params,
        cost_estimate=cost(columns * tok * (PADDED + LATENT), queries.size * 2 + d_out.size * 2),
        name="own_scores",
    )(*kernel_in)
    d_raw, d_gate_t, early_keep, own_keep, send = pl.pallas_call(
        grads,
        out_shape=[
            kept((columns, tok), BF16),
            jax.ShapeDtypeStruct((heads, tok), F32),
            kept((half, tok), F32),
            kept((half, tok), F32),
            kept((half, 2 * tok), BF16),
        ],
        in_specs=[vmem] * 10,
        out_specs=[vmem] * 5,
        scratch_shapes=[
            pltpu.VMEM((WIDTH, 4 * late * tok), BF16),
            pltpu.VMEM((LATENT, 4 * late * tok), BF16),
            pltpu.VMEM((columns, tok), BF16),
            pltpu.VMEM((WIDTH, 2 * tok), F32),
        ],
        compiler_params=params,
        cost_estimate=cost(3 * columns * tok * (WIDTH + LATENT), 0),
        name="grads",
    )(own_s, own_d, q_turned, g_turned, q_late, g_late, prior_t, keys_t, gate_t, ids)
    group = lax.axis_size("head")

    def exchanged(value, step):
        return lax.ppermute(value, "head", [(i, i ^ step) for i in range(group)])

    def small(kernel, name, *operands):
        return pl.pallas_call(
            kernel,
            out_shape=kept((half, tok), BF16),
            in_specs=[vmem] * len(operands),
            out_specs=vmem,
            compiler_params=params,
            name=name,
        )(*operands)

    def query_part(first, count, after, *rest):
        return pl.pallas_call(
            functools.partial(query_grads, first),
            out_shape=[jax.ShapeDtypeStruct(queries.shape, queries.dtype), kept((8, 128), F32)],
            in_specs=[vmem] * 3 + [hbm] * (1 + len(rest)),
            out_specs=[hbm, vmem],
            scratch_shapes=[pltpu.VMEM((count * 2 * tok, PAIR), BF16), pltpu.SemaphoreType.DMA((2 * count,))],
            input_output_aliases={4: 0} if rest else {},
            compiler_params=params,
            cost_estimate=cost(count * 8 * tok * tok * PADDED, count * 4 * tok * PAIR),
            name="query_grads",
        )(d_raw, prior_t, keys_t, after, *rest)

    sent = exchanged(send, 1)
    returned = shifted(small(add_early, "add_early", early_keep, sent), "ctx", -1)
    cut = (quads + 1) // 2
    d_queries, done = query_part(0, cut, sent)
    total = small(add_own, "add_own", own_keep, sent, returned, done)
    d_queries, done = query_part(cut, quads - cut, total, d_queries)
    step = 2
    while step < group:
        total = small(add_halves, "add_halves", total, exchanged(total, step), done)
        step *= 2
    other = exchanged(total, 1)
    first = lax.axis_index("head") % 2 == 0
    d_latent_t = jnp.where(first, jnp.concatenate([total, other]), jnp.concatenate([other, total])).astype(F32)
    return d_queries, d_gate_t.T, d_latent_t.T


def solution(mesh):
    placed = (P("ctx", "head"), P("ctx", None), P("ctx", "head"), P("ctx", "head"), P())
    return jax.shard_map(
        shards,
        mesh=mesh,
        in_specs=placed,
        out_specs=(P("ctx", "head"), P("ctx", "head"), P("ctx", None)),
        check_vma=False,
    )
```

```python
import functools

import jax
import jax.numpy as jnp
from jax import lax
from jax.experimental import pallas as pl
from jax.experimental.pallas import tpu as pltpu
from jax.sharding import PartitionSpec as P

LATENT = 512
ROPE = 64
WIDTH = LATENT + ROPE
PAIR = 2 * WIDTH
PADDED = LATENT + 2 * ROPE
SCALE = 192.0 ** (-0.5)
CAP = 20.0
LOG2_E = 1.4426950408889634
LANES = 128
TILE = 256
AHEAD = 3
EARLY = 4
BF16 = jnp.bfloat16
F32 = jnp.float32


def dot_nn(a, b):
    return lax.dot_general(a, b, (((1,), (0,)), ((), ())), preferred_element_type=F32)


def padded_keys(keys_t):
    spare = jnp.zeros((ROPE, keys_t.shape[1]), keys_t.dtype)
    even = jnp.concatenate([keys_t, spare], axis=0).T
    odd = jnp.concatenate([spare, keys_t], axis=0).T
    return even, odd


def latent_grad_t(even, odd, values):
    first = even + jnp.concatenate([values, jnp.zeros((values.shape[0], 2 * ROPE), F32)], axis=1)
    return first.T[:WIDTH] + odd.T[ROPE:]


def query_tile(q, block, odd):
    size = 2 * TILE * WIDTH // q.shape[1]
    rows, at = pl.ds(block * size, size), LATENT if odd else 0
    pairs = TILE // size
    return jnp.concatenate([q[rows, pl.ds(p * PAIR + at, PADDED)] for p in range(pairs)], axis=0)


def cotangent_tile(g, block, odd):
    size = 2 * TILE * LATENT // g.shape[1]
    rows = pl.ds(block * size, size)
    pairs = TILE // size
    return jnp.concatenate([g[rows, pl.ds((2 * p + odd) * LATENT, LATENT)] for p in range(pairs)], axis=0)


def turn(q, g, block, odd, q_turned, g_turned, start):
    cols = pl.ds(start, TILE)
    turned = query_tile(q, block, odd).T
    q_turned[:, cols] = turned[ROPE:] if odd else turned[:WIDTH]
    g_turned[:, cols] = cotangent_tile(g, block, odd).T


def spread(value, block, size):
    lane = lax.broadcasted_iota(jnp.int32, value.shape, 1)
    value = jnp.where(lane // size == block, value, jnp.zeros_like(value))
    shift = size
    while shift < value.shape[1]:
        value = value + pltpu.roll(value, shift, 1)
        shift *= 2
    return value


def head_of(shape, odd, part, size):
    return 2 * (part * (LANES // size) + lax.broadcasted_iota(jnp.int32, shape, 1) // size) + odd


def load(q_hbm, g_hbm, keys_hbm, q, g, q_turned, g_turned, keys_t, sems, key_sem):
    tok, heads = q.shape[0], g.shape[1] // LATENT
    size = 2 * TILE // heads
    blocks, early = tok // size, q_turned.shape[1] // (2 * TILE)
    keys_copy = pltpu.make_async_copy(keys_hbm, keys_t, key_sem.at[0])
    keys_copy.start()

    def copies(block):
        rows = pl.ds(block * size, size)
        return [
            pltpu.make_async_copy(s.at[rows, :], d.at[rows, :], sems.at[block, n])
            for n, (s, d) in enumerate(((q_hbm, q), (g_hbm, g)))
        ]

    for block in range(min(AHEAD, blocks)):
        for copy in copies(block):
            copy.start()
    for block in range(blocks):
        if block + AHEAD < blocks:
            for copy in copies(block + AHEAD):
                copy.start()
        for copy in copies(block):
            copy.wait()
        if block < early:
            for odd in (0, 1):
                turn(q, g, block, odd, q_turned, g_turned, (2 * block + odd) * TILE)
    keys_copy.wait()


def grads(
    q, g, q_turned, g_turned, prior_t, keys_t, gate_t, segments,
    d_raw, gate_rows, early_keep, own_keep, send,
    q_turned_late, g_turned_late, acc_even, acc_odd, acc_val, whole,
):
    tok, heads = gate_t.shape[1], gate_t.shape[0]
    size = 2 * TILE // heads
    window = tok + size
    blocks, early = tok // size, q_turned.shape[1] // (2 * TILE)
    shard = lax.axis_index("ctx")
    keys = jnp.concatenate([prior_t[...].T, keys_t[...].T], axis=0)
    row_own = segments[pl.ds(shard, 1), :]
    row_prior = segments[pl.ds(jnp.maximum(shard - 1, 0), 1), :]
    key_segment = jnp.concatenate(
        [jnp.broadcast_to(row_prior, (tok, tok)).T, jnp.broadcast_to(row_own, (tok, tok)).T], axis=0
    )
    for acc in (acc_even, acc_odd, acc_val):
        acc[...] = jnp.zeros_like(acc)

    def keys_of(block):
        return pl.ds(block * size, window)

    def allowed_in(block):
        key_at = block * size + lax.broadcasted_iota(jnp.int32, (window, tok), 0)
        query_at = block * size + lax.broadcasted_iota(jnp.int32, (window, tok), 1) % size
        query_segment = spread(jnp.broadcast_to(row_own, (8, tok)), block, size)[:1]
        same = key_segment[block * size : block * size + window] == query_segment
        allowed = same & (key_at - tok <= query_at) & ((key_at >= tok) | (shard > 0))
        return jnp.concatenate([allowed, allowed], axis=1)

    def gates_of(block, odd):
        spread_gate = spread(gate_t[...], block, size)
        head = lax.broadcasted_iota(jnp.int32, spread_gate.shape, 0)
        return jnp.concatenate(
            [
                jnp.sum(
                    jnp.where(head == head_of(spread_gate.shape, odd, part, size), spread_gate, 0.0),
                    axis=0,
                    keepdims=True,
                )
                for part in range(TILE // LANES)
            ],
            axis=1,
        )

    def scores_of(n):
        block = n // 2
        if block < early:
            q_from, g_from, cols = q_turned, g_turned, pl.ds(n * TILE, TILE)
        else:
            q_from, g_from, cols = q_turned_late, g_turned_late, pl.ds((n - 2 * early) * TILE, TILE)
        held = keys[block * size : block * size + window]
        return dot_nn(held, q_from[:, cols]), dot_nn(held[:, :LATENT], g_from[:, cols])

    def softmax_of(n, raw, d_p, allowed):
        squashed = jnp.tanh(raw * (SCALE / CAP))
        weights = jnp.where(allowed, jnp.exp2((CAP * LOG2_E) * squashed), 0.0)
        opened = jax.nn.sigmoid(gates_of(n // 2, n % 2))
        inverse = 1.0 / jnp.sum(weights, axis=0, keepdims=True)
        mean = jnp.sum(weights * d_p, axis=0, keepdims=True) * inverse
        gate_rows[pl.ds(n, 1), :] = opened * (1.0 - opened) * mean
        gated = weights * (inverse * opened)
        slope = gated * (d_p - mean) * (SCALE - SCALE * squashed * squashed)
        d_raw[pl.ds(n * window, window), :] = slope.astype(BF16)
        return gated.astype(BF16)

    def add_up(n, gated):
        block, odd = n // 2, n % 2
        acc = acc_odd if odd else acc_even
        acc[keys_of(block), :] += dot_nn(d_raw[pl.ds(n * window, window), :], query_tile(q, block, odd))
        acc_val[keys_of(block), :] += dot_nn(gated, cotangent_tile(g, block, odd))

    count = 2 * blocks
    raws, gateds = {}, {}
    turned = 2 * early
    for n in range(count + 2):
        while turned < min(count, n + 2):
            turn(q, g, turned // 2, turned % 2, q_turned_late, g_turned_late, (turned - 2 * early) * TILE)
            turned += 1
        if n < count:
            raws[n] = scores_of(n)
        if 1 <= n <= count:
            if n % 2:
                allowed = allowed_in((n - 1) // 2)
            gateds[n - 1] = softmax_of(n - 1, *raws.pop(n - 1), allowed)
        if n >= 2:
            add_up(n - 2, gateds.pop(n - 2))
    whole[...] = latent_grad_t(acc_even[...], acc_odd[...], acc_val[...])
    core = lax.axis_index("head") % 2
    half = WIDTH // 2
    mine = pl.ds(pl.multiple_of(core * half, 32), half)
    others = pl.ds(pl.multiple_of((1 - core) * half, 32), half)
    early_keep[...] = whole[mine, :tok]
    own_keep[...] = whole[mine, tok:]
    send[...] = whole[others, :].astype(send.dtype)


def query_grads(first_block, d_raw, prior_t, keys_t, gate_rows, after, *refs):
    stage, sems = refs[-2:]
    if first_block == 0:
        out_hbm, done, d_gate = refs[-5:-2]
    else:
        out_hbm, done = refs[-4:-2]
    tok = keys_t.shape[1]
    heads = stage.shape[1] // WIDTH
    size = 2 * TILE // heads
    window = tok + size
    pairs = TILE // size
    even_prior, odd_prior = padded_keys(prior_t[...])
    even_own, odd_own = padded_keys(keys_t[...])
    even = jnp.concatenate([even_prior, even_own], axis=0)
    odd = jnp.concatenate([odd_prior, odd_own], axis=0)
    copies = []
    for at in range(stage.shape[0] // size):
        block = first_block + at
        low, high = block * size, block * size + window
        slopes = [d_raw[pl.ds((2 * block + n) * window, window), :].T for n in range(2)]
        middle = jnp.concatenate([even[low:high, LATENT:], odd[low:high, : 2 * ROPE]], axis=0)
        for column, part in (
            (0, dot_nn(slopes[0], even[low:high, :LATENT])),
            (LATENT, dot_nn(jnp.concatenate(slopes, axis=1), middle)),
            (LATENT + 2 * ROPE, dot_nn(slopes[1], odd[low:high, 2 * ROPE :])),
        ):
            part = part.astype(BF16)
            for p in range(pairs):
                stage[pl.ds(at * size, size), pl.ds(p * PAIR + column, part.shape[1])] = part[
                    p * size : (p + 1) * size
                ]
        copies.append(
            pltpu.make_async_copy(
                stage.at[pl.ds(at * size, size), :], out_hbm.at[pl.ds(low, size), :], sems.at[at]
            )
        )
        copies[-1].start()
    if first_block == 0:
        shape = d_gate.shape
        head = lax.broadcasted_iota(jnp.int32, shape, 0)
        lane = lax.broadcasted_iota(jnp.int32, shape, 1)
        found = jnp.zeros(shape, F32)
        for block in range(tok // size):
            value = jnp.zeros(shape, F32)
            for n in range(2):
                row = gate_rows[pl.ds(2 * block + n, 1), :]
                for part in range(TILE // LANES):
                    held = jnp.broadcast_to(row[:, part * LANES : (part + 1) * LANES], shape)
                    value = jnp.where(head == head_of(shape, n, part, size), held, value)
            shift = size
            while shift < tok:
                value = value + pltpu.roll(value, shift, 1)
                shift *= 2
            found = jnp.where(lane // size == block, value, found)
        d_gate[...] = found
    for copy in copies:
        copy.wait()
    done[...] = jnp.zeros_like(done)


def add_early(keep, other, out):
    out[...] = (keep[...] + other[:, : out.shape[1]].astype(F32)).astype(out.dtype)


def add_own(keep, other, returned, after, out):
    out[...] = (keep[...] + other[:, out.shape[1] :].astype(F32) + returned[...].astype(F32)).astype(out.dtype)


def add_halves(a, b, after, out):
    out[...] = (a[...].astype(F32) + b[...].astype(F32)).astype(out.dtype)


def shifted(value, axis, steps):
    count = lax.axis_size(axis)
    first, last = (max(0, -steps), min(count, count - steps))
    return lax.ppermute(value, axis, [(source, source + steps) for source in range(first, last)])


def shards(queries, latent, gate, d_out, segments):
    tok = latent.shape[0]
    heads = gate.shape[1]
    size = 2 * TILE // heads
    window = tok + size
    blocks = tok // size
    early = max(1, blocks * EARLY // 8)
    half = WIDTH // 2
    columns = heads * tok
    vmem = pl.BlockSpec(memory_space=pltpu.VMEM)
    hbm = pl.BlockSpec(memory_space=pl.ANY)
    params = pltpu.CompilerParams(vmem_limit_bytes=28 * 1024 * 1024)
    kept = pltpu.VMEM
    keys_t = latent.T
    gate_t = gate.T
    ids = segments.reshape(-1, tok)

    def cost(multiply_adds, moved):
        return pl.CostEstimate(flops=2 * multiply_adds, bytes_accessed=moved, transcendentals=0)

    prior_t = shifted(keys_t, "ctx", 1)
    q, g, q_turned, g_turned, keys_t = pl.pallas_call(
        load,
        out_shape=[
            kept(queries.shape, BF16),
            kept(d_out.shape, BF16),
            kept((WIDTH, 2 * early * TILE), BF16),
            kept((LATENT, 2 * early * TILE), BF16),
            kept((WIDTH, tok), BF16),
        ],
        in_specs=[hbm] * 3,
        out_specs=[vmem] * 5,
        scratch_shapes=[pltpu.SemaphoreType.DMA((blocks, 2)), pltpu.SemaphoreType.DMA((1,))],
        compiler_params=params,
        cost_estimate=cost(0, queries.size * 2 + d_out.size * 2),
        name="load",
    )(*[pltpu.with_memory_space_constraint(x, pltpu.HBM) for x in (queries, d_out, keys_t)])
    d_raw, gate_rows, early_keep, own_keep, send = pl.pallas_call(
        grads,
        out_shape=[
            kept((2 * blocks * window, TILE), BF16),
            kept((2 * blocks, TILE), F32),
            kept((half, tok), F32),
            kept((half, tok), F32),
            kept((half, 2 * tok), BF16),
        ],
        in_specs=[vmem] * 8,
        out_specs=[vmem] * 5,
        scratch_shapes=[
            pltpu.VMEM((WIDTH, 2 * (blocks - early) * TILE), BF16),
            pltpu.VMEM((LATENT, 2 * (blocks - early) * TILE), BF16),
            pltpu.VMEM((2 * tok, PADDED), F32),
            pltpu.VMEM((2 * tok, PADDED), F32),
            pltpu.VMEM((2 * tok, LATENT), F32),
            pltpu.VMEM((WIDTH, 2 * tok), F32),
        ],
        compiler_params=params,
        cost_estimate=cost(2 * columns * window * (WIDTH + LATENT), 0),
        name="grads",
    )(q, g, q_turned, g_turned, prior_t, keys_t, gate_t, ids)
    group = lax.axis_size("head")

    def exchanged(value, step):
        return lax.ppermute(value, "head", [(i, i ^ step) for i in range(group)])

    def small(kernel, name, *operands):
        return pl.pallas_call(
            kernel,
            out_shape=kept((half, tok), BF16),
            in_specs=[vmem] * len(operands),
            out_specs=vmem,
            compiler_params=params,
            name=name,
        )(*operands)

    def query_part(first, count, after, *rest):
        d_gate = [] if rest else [jax.ShapeDtypeStruct((heads, tok), F32)]
        return pl.pallas_call(
            functools.partial(query_grads, first),
            out_shape=[jax.ShapeDtypeStruct(queries.shape, queries.dtype), kept((8, 128), F32)] + d_gate,
            in_specs=[vmem] * 4 + [hbm] * (1 + len(rest)),
            out_specs=[hbm, vmem] + [vmem] * len(d_gate),
            scratch_shapes=[
                pltpu.VMEM((count * size, queries.shape[1]), BF16),
                pltpu.SemaphoreType.DMA((count,)),
            ],
            input_output_aliases={5: 0} if rest else {},
            compiler_params=params,
            cost_estimate=cost(count * 2 * TILE * window * PADDED, count * size * queries.shape[1] * 2),
            name="query_grads",
        )(d_raw, prior_t, keys_t, gate_rows, after, *rest)

    sent = exchanged(send, 1)
    returned = shifted(small(add_early, "add_early", early_keep, sent), "ctx", -1)
    cut = (blocks + 1) // 2
    d_queries, done, d_gate_t = query_part(0, cut, sent)
    total = small(add_own, "add_own", own_keep, sent, returned, done)
    d_queries, done = query_part(cut, blocks - cut, total, d_queries)
    step = 2
    while step < group:
        total = small(add_halves, "add_halves", total, exchanged(total, step), done)
        step *= 2
    other = exchanged(total, 1)
    first = lax.axis_index("head") % 2 == 0
    d_latent_t = jnp.where(first, jnp.concatenate([total, other]), jnp.concatenate([other, total])).astype(F32)
    return d_queries, d_gate_t.T, d_latent_t.T


def solution(mesh):
    placed = (P("ctx", "head"), P("ctx", None), P("ctx", "head"), P("ctx", "head"), P())
    return jax.shard_map(
        shards,
        mesh=mesh,
        in_specs=placed,
        out_specs=(P("ctx", "head"), P("ctx", "head"), P("ctx", None)),
        check_vma=False,
    )
```

```python
import functools

import jax
import jax.numpy as jnp
from jax import lax
from jax.experimental import pallas as pl
from jax.experimental.pallas import tpu as pltpu
from jax.sharding import PartitionSpec as P

LATENT = 512
ROPE = 64
WIDTH = LATENT + ROPE
PAIR = 2 * WIDTH
PADDED = LATENT + 2 * ROPE
SCALE = 192.0 ** (-0.5)
CAP = 20.0
LOG2_E = 1.4426950408889634
LANES = 128
TILE = 256
AHEAD = 8
EARLY = 7
BF16 = jnp.bfloat16
F32 = jnp.float32


def dot_nn(a, b):
    return lax.dot_general(a, b, (((1,), (0,)), ((), ())), preferred_element_type=F32)


def padded_keys(keys_t):
    spare = jnp.zeros((ROPE, keys_t.shape[1]), keys_t.dtype)
    even = jnp.concatenate([keys_t, spare], axis=0).T
    odd = jnp.concatenate([spare, keys_t], axis=0).T
    return even, odd


def latent_grad_t(even, odd, values):
    first = even + jnp.concatenate([values, jnp.zeros((values.shape[0], 2 * ROPE), F32)], axis=1)
    return first.T[:WIDTH] + odd.T[ROPE:]


def query_tile(q, block, odd):
    size = 2 * TILE * WIDTH // q.shape[1]
    rows, at = pl.ds(block * size, size), LATENT if odd else 0
    pairs = TILE // size
    return jnp.concatenate([q[rows, pl.ds(p * PAIR + at, PADDED)] for p in range(pairs)], axis=0)


def cotangent_tile(g, block, odd):
    size = 2 * TILE * LATENT // g.shape[1]
    rows = pl.ds(block * size, size)
    pairs = TILE // size
    return jnp.concatenate([g[rows, pl.ds((2 * p + odd) * LATENT, LATENT)] for p in range(pairs)], axis=0)


def turn(q, g, block, odd, q_turned, g_turned, start):
    cols = pl.ds(start, TILE)
    turned = query_tile(q, block, odd).T
    q_turned[:, cols] = turned[ROPE:] if odd else turned[:WIDTH]
    g_turned[:, cols] = cotangent_tile(g, block, odd).T


def spread(value, block, size):
    lane = lax.broadcasted_iota(jnp.int32, value.shape, 1)
    value = jnp.where(lane // size == block, value, jnp.zeros_like(value))
    shift = size
    while shift < value.shape[1]:
        value = value + pltpu.roll(value, shift, 1)
        shift *= 2
    return value


def head_of(shape, odd, part, size):
    return 2 * (part * (LANES // size) + lax.broadcasted_iota(jnp.int32, shape, 1) // size) + odd


def load(q_hbm, g_hbm, keys_hbm, q, g, q_turned, g_turned, keys_t, sems, key_sem):
    tok, heads = q.shape[0], g.shape[1] // LATENT
    size = 2 * TILE // heads
    blocks, early = tok // size, q_turned.shape[1] // (2 * TILE)
    keys_copy = pltpu.make_async_copy(keys_hbm, keys_t, key_sem.at[0])
    keys_copy.start()

    def copies(block):
        rows = pl.ds(block * size, size)
        return [
            pltpu.make_async_copy(s.at[rows, :], d.at[rows, :], sems.at[block, n])
            for n, (s, d) in enumerate(((q_hbm, q), (g_hbm, g)))
        ]

    for block in range(min(AHEAD, blocks)):
        for copy in copies(block):
            copy.start()
    for block in range(blocks):
        if block + AHEAD < blocks:
            for copy in copies(block + AHEAD):
                copy.start()
        for copy in copies(block):
            copy.wait()
        if block < early:
            for odd in (0, 1):
                turn(q, g, block, odd, q_turned, g_turned, (2 * block + odd) * TILE)
    keys_copy.wait()


def grads(
    q, g, q_turned, g_turned, prior_t, keys_t, gate_t, segments,
    d_raw, gate_rows, early_keep, own_keep, send,
    q_turned_late, g_turned_late, acc_even, acc_odd, acc_val, whole,
):
    tok, heads = gate_t.shape[1], gate_t.shape[0]
    size = 2 * TILE // heads
    window = tok + size
    blocks, early = tok // size, q_turned.shape[1] // (2 * TILE)
    shard = lax.axis_index("ctx")
    keys = jnp.concatenate([prior_t[...].T, keys_t[...].T], axis=0)
    row_own = segments[pl.ds(shard, 1), :]
    row_prior = segments[pl.ds(jnp.maximum(shard - 1, 0), 1), :]
    key_segment = jnp.concatenate(
        [jnp.broadcast_to(row_prior, (tok, tok)).T, jnp.broadcast_to(row_own, (tok, tok)).T], axis=0
    )
    for acc in (acc_even, acc_odd, acc_val):
        acc[...] = jnp.zeros_like(acc)

    def keys_of(block):
        return pl.ds(block * size, window)

    def allowed_in(block):
        key_at = block * size + lax.broadcasted_iota(jnp.int32, (window, tok), 0)
        query_at = block * size + lax.broadcasted_iota(jnp.int32, (window, tok), 1) % size
        query_segment = spread(jnp.broadcast_to(row_own, (8, tok)), block, size)[:1]
        same = key_segment[block * size : block * size + window] == query_segment
        allowed = same & (key_at - tok <= query_at) & ((key_at >= tok) | (shard > 0))
        return allowed

    def gates_of(block, odd):
        spread_gate = spread(gate_t[...], block, size)
        head = lax.broadcasted_iota(jnp.int32, spread_gate.shape, 0)
        return jnp.concatenate(
            [
                jnp.sum(
                    jnp.where(head == head_of(spread_gate.shape, odd, part, size), spread_gate, 0.0),
                    axis=0,
                    keepdims=True,
                )
                for part in range(TILE // LANES)
            ],
            axis=1,
        )

    def scores_of(n):
        block = n // 2
        if block < early:
            q_from, g_from, cols = q_turned, g_turned, pl.ds(n * TILE, TILE)
        else:
            q_from, g_from, cols = q_turned_late, g_turned_late, pl.ds((n - 2 * early) * TILE, TILE)
        held = keys[block * size : block * size + window]
        return dot_nn(held, q_from[:, cols]), dot_nn(held[:, :LATENT], g_from[:, cols])

    def softmax_of(n, raw, d_p, allowed):
        gate = gates_of(n // 2, n % 2)
        gateds = []
        for part in range(TILE // LANES):
            lanes = slice(part * LANES, (part + 1) * LANES)
            squashed = jnp.tanh(raw[:, lanes] * (SCALE / CAP))
            weights = jnp.where(allowed, jnp.exp2((CAP * LOG2_E) * squashed), 0.0)
            opened = jax.nn.sigmoid(gate[:, lanes])
            inverse = 1.0 / jnp.sum(weights, axis=0, keepdims=True)
            mean = jnp.sum(weights * d_p[:, lanes], axis=0, keepdims=True) * inverse
            gate_rows[pl.ds(n, 1), pl.ds(part * LANES, LANES)] = opened * (1.0 - opened) * mean
            gated = weights * (inverse * opened)
            slope = gated * (d_p[:, lanes] - mean) * (SCALE - SCALE * squashed * squashed)
            d_raw[pl.ds(n * window, window), pl.ds(part * LANES, LANES)] = slope.astype(BF16)
            gateds.append(gated.astype(BF16))
        return jnp.concatenate(gateds, axis=1)

    def add_up(n, gated):
        block, odd = n // 2, n % 2
        acc = acc_odd if odd else acc_even
        acc[keys_of(block), :] += dot_nn(d_raw[pl.ds(n * window, window), :], query_tile(q, block, odd))
        acc_val[keys_of(block), :] += dot_nn(gated, cotangent_tile(g, block, odd))

    count = 2 * blocks
    raws, gateds = {}, {}
    turned = 2 * early
    for n in range(count + 2):
        while turned < min(count, n + 2):
            turn(q, g, turned // 2, turned % 2, q_turned_late, g_turned_late, (turned - 2 * early) * TILE)
            turned += 1
        if n < count:
            raws[n] = scores_of(n)
        if 1 <= n <= count:
            if n % 2:
                allowed = allowed_in((n - 1) // 2)
            gateds[n - 1] = softmax_of(n - 1, *raws.pop(n - 1), allowed)
        if n >= 2:
            add_up(n - 2, gateds.pop(n - 2))
    odd_moved = pltpu.roll(acc_odd[...], PADDED - ROPE, 1)
    summed = acc_even[...] + odd_moved + jnp.concatenate([acc_val[...], jnp.zeros((2 * tok, 2 * ROPE), F32)], axis=1)
    whole[...] = summed.astype(BF16).T[:WIDTH]
    core = lax.axis_index("head") % 2
    half = WIDTH // 2
    mine = pl.ds(pl.multiple_of(core * half, 32), half)
    others = pl.ds(pl.multiple_of((1 - core) * half, 32), half)
    early_keep[...] = whole[mine, :tok]
    own_keep[...] = whole[mine, tok:]
    send[...] = whole[others, :]


def query_grads(first_block, d_raw, prior_t, keys_t, gate_rows, after, *refs):
    stage, sems = refs[-2:]
    if first_block == 0:
        out_hbm, done, d_gate = refs[-5:-2]
    else:
        out_hbm, done = refs[-4:-2]
    tok = keys_t.shape[1]
    heads = stage.shape[1] // WIDTH
    size = 2 * TILE // heads
    window = tok + size
    pairs = TILE // size
    even_prior, odd_prior = padded_keys(prior_t[...])
    even_own, odd_own = padded_keys(keys_t[...])
    even = jnp.concatenate([even_prior, even_own], axis=0)
    odd = jnp.concatenate([odd_prior, odd_own], axis=0)
    copies = []
    for at in range(stage.shape[0] // size):
        block = first_block + at
        low, high = block * size, block * size + window
        slopes = [d_raw[pl.ds((2 * block + n) * window, window), :].T for n in range(2)]
        middle = jnp.concatenate([even[low:high, LATENT:], odd[low:high, : 2 * ROPE]], axis=0)
        for column, part in (
            (0, dot_nn(slopes[0], even[low:high, :LATENT])),
            (LATENT, dot_nn(jnp.concatenate(slopes, axis=1), middle)),
            (LATENT + 2 * ROPE, dot_nn(slopes[1], odd[low:high, 2 * ROPE :])),
        ):
            part = part.astype(BF16)
            for p in range(pairs):
                stage[pl.ds(at * size, size), pl.ds(p * PAIR + column, part.shape[1])] = part[
                    p * size : (p + 1) * size
                ]
        copies.append(
            pltpu.make_async_copy(
                stage.at[pl.ds(at * size, size), :], out_hbm.at[pl.ds(low, size), :], sems.at[at]
            )
        )
        copies[-1].start()
    if first_block == 0:
        shape = d_gate.shape
        head = lax.broadcasted_iota(jnp.int32, shape, 0)
        lane = lax.broadcasted_iota(jnp.int32, shape, 1)
        found = jnp.zeros(shape, F32)
        for block in range(tok // size):
            value = jnp.zeros(shape, F32)
            for n in range(2):
                row = gate_rows[pl.ds(2 * block + n, 1), :]
                for part in range(TILE // LANES):
                    held = jnp.broadcast_to(row[:, part * LANES : (part + 1) * LANES], shape)
                    value = jnp.where(head == head_of(shape, n, part, size), held, value)
            shift = size
            while shift < tok:
                value = value + pltpu.roll(value, shift, 1)
                shift *= 2
            found = jnp.where(lane // size == block, value, found)
        d_gate[...] = found
    for copy in copies:
        copy.wait()
    done[...] = jnp.zeros_like(done)


def add_early(keep, other, out):
    out[...] = (keep[...].astype(F32) + other[:, : out.shape[1]].astype(F32)).astype(out.dtype)


def add_own(keep, other, returned, after, out):
    out[...] = (keep[...].astype(F32) + other[:, out.shape[1] :].astype(F32) + returned[...].astype(F32)).astype(out.dtype)


def add_halves(a, b, after, out):
    out[...] = (a[...].astype(F32) + b[...].astype(F32)).astype(out.dtype)


def shifted(value, axis, steps):
    count = lax.axis_size(axis)
    first, last = (max(0, -steps), min(count, count - steps))
    return lax.ppermute(value, axis, [(source, source + steps) for source in range(first, last)])


def shards(queries, latent, gate, d_out, segments):
    tok = latent.shape[0]
    heads = gate.shape[1]
    size = 2 * TILE // heads
    window = tok + size
    blocks = tok // size
    early = max(1, blocks * EARLY // 8)
    half = WIDTH // 2
    columns = heads * tok
    vmem = pl.BlockSpec(memory_space=pltpu.VMEM)
    hbm = pl.BlockSpec(memory_space=pl.ANY)
    params = pltpu.CompilerParams(vmem_limit_bytes=28 * 1024 * 1024)
    kept = pltpu.VMEM
    keys_t = latent.T
    gate_t = gate.T
    ids = segments.reshape(-1, tok)

    def cost(multiply_adds, moved):
        return pl.CostEstimate(flops=2 * multiply_adds, bytes_accessed=moved, transcendentals=0)

    prior_t = shifted(keys_t, "ctx", 1)
    q, g, q_turned, g_turned, keys_t = pl.pallas_call(
        load,
        out_shape=[
            kept(queries.shape, BF16),
            kept(d_out.shape, BF16),
            kept((WIDTH, 2 * early * TILE), BF16),
            kept((LATENT, 2 * early * TILE), BF16),
            kept((WIDTH, tok), BF16),
        ],
        in_specs=[hbm] * 3,
        out_specs=[vmem] * 5,
        scratch_shapes=[pltpu.SemaphoreType.DMA((blocks, 2)), pltpu.SemaphoreType.DMA((1,))],
        compiler_params=params,
        cost_estimate=cost(0, queries.size * 2 + d_out.size * 2),
        name="load",
    )(*[pltpu.with_memory_space_constraint(x, pltpu.HBM) for x in (queries, d_out, keys_t)])
    d_raw, gate_rows, early_keep, own_keep, send = pl.pallas_call(
        grads,
        out_shape=[
            kept((2 * blocks * window, TILE), BF16),
            kept((2 * blocks, TILE), F32),
            kept((half, tok), BF16),
            kept((half, tok), BF16),
            kept((half, 2 * tok), BF16),
        ],
        in_specs=[vmem] * 8,
        out_specs=[vmem] * 5,
        scratch_shapes=[
            pltpu.VMEM((WIDTH, max(1, 2 * (blocks - early)) * TILE), BF16),
            pltpu.VMEM((LATENT, max(1, 2 * (blocks - early)) * TILE), BF16),
            pltpu.VMEM((2 * tok, PADDED), F32),
            pltpu.VMEM((2 * tok, PADDED), F32),
            pltpu.VMEM((2 * tok, LATENT), F32),
            pltpu.VMEM((WIDTH, 2 * tok), BF16),
        ],
        compiler_params=params,
        cost_estimate=cost(2 * columns * window * (WIDTH + LATENT), 0),
        name="grads",
    )(q, g, q_turned, g_turned, prior_t, keys_t, gate_t, ids)
    group = lax.axis_size("head")

    def exchanged(value, step):
        return lax.ppermute(value, "head", [(i, i ^ step) for i in range(group)])

    def small(kernel, name, *operands):
        return pl.pallas_call(
            kernel,
            out_shape=kept((half, tok), BF16),
            in_specs=[vmem] * len(operands),
            out_specs=vmem,
            compiler_params=params,
            name=name,
        )(*operands)

    def query_part(first, count, after, *rest):
        d_gate = [] if rest else [jax.ShapeDtypeStruct((heads, tok), F32)]
        return pl.pallas_call(
            functools.partial(query_grads, first),
            out_shape=[jax.ShapeDtypeStruct(queries.shape, queries.dtype), kept((8, 128), F32)] + d_gate,
            in_specs=[vmem] * 4 + [hbm] * (1 + len(rest)),
            out_specs=[hbm, vmem] + [vmem] * len(d_gate),
            scratch_shapes=[
                pltpu.VMEM((count * size, queries.shape[1]), BF16),
                pltpu.SemaphoreType.DMA((count,)),
            ],
            input_output_aliases={5: 0} if rest else {},
            compiler_params=params,
            cost_estimate=cost(count * 2 * TILE * window * PADDED, count * size * queries.shape[1] * 2),
            name="query_grads",
        )(d_raw, prior_t, keys_t, gate_rows, after, *rest)

    sent = exchanged(send, 1)
    returned = shifted(small(add_early, "add_early", early_keep, sent), "ctx", -1)
    cut = (blocks + 1) // 2
    d_queries, done, d_gate_t = query_part(0, cut, sent)
    total = small(add_own, "add_own", own_keep, sent, returned, done)
    d_queries, done = query_part(cut, blocks - cut, total, d_queries)
    step = 2
    while step < group:
        total = small(add_halves, "add_halves", total, exchanged(total, step), done)
        step *= 2
    other = exchanged(total, 1)
    first = lax.axis_index("head") % 2 == 0
    d_latent_t = jnp.where(first, jnp.concatenate([total, other]), jnp.concatenate([other, total])).astype(F32)
    return d_queries, d_gate_t.T, d_latent_t.T


def solution(mesh):
    placed = (P("ctx", "head"), P("ctx", None), P("ctx", "head"), P("ctx", "head"), P())
    return jax.shard_map(
        shards,
        mesh=mesh,
        in_specs=placed,
        out_specs=(P("ctx", "head"), P("ctx", "head"), P("ctx", None)),
        check_vma=False,
    )
```

```python
import functools

import jax
import jax.numpy as jnp
from jax import lax
from jax.experimental import pallas as pl
from jax.experimental.pallas import tpu as pltpu
from jax.sharding import PartitionSpec as P

LATENT = 512
ROPE = 64
WIDTH = LATENT + ROPE
PAIR = 2 * WIDTH
PADDED = LATENT + 2 * ROPE
SCALE = 192.0 ** (-0.5)
CAP = 20.0
LOG2_E = 1.4426950408889634
LANES = 128
TILE = 256
AHEAD = 8
EARLY = 7
BF16 = jnp.bfloat16
F32 = jnp.float32


def dot_nn(a, b):
    return lax.dot_general(a, b, (((1,), (0,)), ((), ())), preferred_element_type=F32)


def padded_keys(keys_t):
    spare = jnp.zeros((ROPE, keys_t.shape[1]), keys_t.dtype)
    even = jnp.concatenate([keys_t, spare], axis=0).T
    odd = jnp.concatenate([spare, keys_t], axis=0).T
    return even, odd


def latent_grad_t(even, odd, values):
    first = even + jnp.concatenate([values, jnp.zeros((values.shape[0], 2 * ROPE), F32)], axis=1)
    return first.T[:WIDTH] + odd.T[ROPE:]


def query_tile(q, block, odd):
    size = 2 * TILE * WIDTH // q.shape[1]
    rows, at = pl.ds(block * size, size), LATENT if odd else 0
    pairs = TILE // size
    return jnp.concatenate([q[rows, pl.ds(p * PAIR + at, PADDED)] for p in range(pairs)], axis=0)


def cotangent_tile(g, block, odd):
    size = 2 * TILE * LATENT // g.shape[1]
    rows = pl.ds(block * size, size)
    pairs = TILE // size
    return jnp.concatenate([g[rows, pl.ds((2 * p + odd) * LATENT, LATENT)] for p in range(pairs)], axis=0)


def turn(q, g, block, odd, q_turned, g_turned, start):
    cols = pl.ds(start, TILE)
    turned = query_tile(q, block, odd).T
    q_turned[:, cols] = turned[ROPE:] if odd else turned[:WIDTH]
    g_turned[:, cols] = cotangent_tile(g, block, odd).T


def spread(value, block, size):
    lane = lax.broadcasted_iota(jnp.int32, value.shape, 1)
    value = jnp.where(lane // size == block, value, jnp.zeros_like(value))
    shift = size
    while shift < value.shape[1]:
        value = value + pltpu.roll(value, shift, 1)
        shift *= 2
    return value


def head_of(shape, odd, part, size):
    return 2 * (part * (LANES // size) + lax.broadcasted_iota(jnp.int32, shape, 1) // size) + odd


def load(q_hbm, g_hbm, keys_hbm, q, g, q_turned, g_turned, keys_t, sems, key_sem):
    tok, heads = q.shape[0], g.shape[1] // LATENT
    size = 2 * TILE // heads
    blocks, early = tok // size, q_turned.shape[1] // (2 * TILE)
    keys_copy = pltpu.make_async_copy(keys_hbm, keys_t, key_sem.at[0])
    keys_copy.start()

    def copies(block):
        rows = pl.ds(block * size, size)
        return [
            pltpu.make_async_copy(s.at[rows, :], d.at[rows, :], sems.at[block, n])
            for n, (s, d) in enumerate(((q_hbm, q), (g_hbm, g)))
        ]

    for block in range(min(AHEAD, blocks)):
        for copy in copies(block):
            copy.start()
    for block in range(blocks):
        if block + AHEAD < blocks:
            for copy in copies(block + AHEAD):
                copy.start()
        for copy in copies(block):
            copy.wait()
        if block < early:
            for odd in (0, 1):
                turn(q, g, block, odd, q_turned, g_turned, (2 * block + odd) * TILE)
    keys_copy.wait()


def grads(
    q, g, q_turned, g_turned, prior_t, keys_t, gate_t, segments,
    d_raw, gate_rows, early_keep, own_keep, send,
    q_turned_late, g_turned_late, acc_even, acc_odd, acc_val, whole,
):
    tok, heads = gate_t.shape[1], gate_t.shape[0]
    size = 2 * TILE // heads
    window = tok + size
    blocks, early = tok // size, q_turned.shape[1] // (2 * TILE)
    shard = lax.axis_index("ctx")
    keys = jnp.concatenate([prior_t[...].T, keys_t[...].T], axis=0)
    row_own = segments[pl.ds(shard, 1), :]
    row_prior = segments[pl.ds(jnp.maximum(shard - 1, 0), 1), :]
    key_segment = jnp.concatenate(
        [jnp.broadcast_to(row_prior, (tok, tok)).T, jnp.broadcast_to(row_own, (tok, tok)).T], axis=0
    )
    for acc in (acc_even, acc_odd, acc_val):
        acc[...] = jnp.zeros_like(acc)

    def keys_of(block):
        return pl.ds(block * size, window)

    def allowed_in(block):
        key_at = block * size + lax.broadcasted_iota(jnp.int32, (window, tok), 0)
        query_at = block * size + lax.broadcasted_iota(jnp.int32, (window, tok), 1) % size
        query_segment = spread(jnp.broadcast_to(row_own, (8, tok)), block, size)[:1]
        same = key_segment[block * size : block * size + window] == query_segment
        allowed = same & (key_at - tok <= query_at) & ((key_at >= tok) | (shard > 0))
        return allowed

    def gates_of(block, odd):
        spread_gate = spread(gate_t[...], block, size)
        head = lax.broadcasted_iota(jnp.int32, spread_gate.shape, 0)
        return jnp.concatenate(
            [
                jnp.sum(
                    jnp.where(head == head_of(spread_gate.shape, odd, part, size), spread_gate, 0.0),
                    axis=0,
                    keepdims=True,
                )
                for part in range(TILE // LANES)
            ],
            axis=1,
        )

    def scores_of(n):
        block = n // 2
        if block < early:
            q_from, g_from, cols = q_turned, g_turned, pl.ds(n * TILE, TILE)
        else:
            q_from, g_from, cols = q_turned_late, g_turned_late, pl.ds((n - 2 * early) * TILE, TILE)
        held = keys[block * size : block * size + window]
        return dot_nn(held, q_from[:, cols]), dot_nn(held[:, :LATENT], g_from[:, cols])

    def softmax_of(n, raw, d_p, allowed):
        gate = gates_of(n // 2, n % 2)
        gateds = []
        for part in range(TILE // LANES):
            lanes = slice(part * LANES, (part + 1) * LANES)
            squashed = jnp.tanh(raw[:, lanes] * (SCALE / CAP))
            weights = jnp.where(allowed, jnp.exp2((CAP * LOG2_E) * squashed), 0.0)
            opened = jax.nn.sigmoid(gate[:, lanes])
            inverse = 1.0 / jnp.sum(weights, axis=0, keepdims=True)
            mean = jnp.sum(weights * d_p[:, lanes], axis=0, keepdims=True) * inverse
            gate_rows[pl.ds(n, 1), pl.ds(part * LANES, LANES)] = opened * (1.0 - opened) * mean
            gated = weights * (inverse * opened)
            slope = weights * (inverse * opened * SCALE) * (d_p[:, lanes] - mean) * (1.0 - squashed * squashed)
            d_raw[pl.ds(n * window, window), pl.ds(part * LANES, LANES)] = slope.astype(BF16)
            gateds.append(gated.astype(BF16))
        return jnp.concatenate(gateds, axis=1)

    def add_up(n, gated):
        block, odd = n // 2, n % 2
        acc = acc_odd if odd else acc_even
        acc[keys_of(block), :] += dot_nn(d_raw[pl.ds(n * window, window), :], query_tile(q, block, odd))
        acc_val[keys_of(block), :] += dot_nn(gated, cotangent_tile(g, block, odd))

    count = 2 * blocks
    raws, gateds = {}, {}
    turned = 2 * early
    for n in range(count + 2):
        while turned < min(count, n + 2):
            turn(q, g, turned // 2, turned % 2, q_turned_late, g_turned_late, (turned - 2 * early) * TILE)
            turned += 1
        if n < count:
            raws[n] = scores_of(n)
        if 1 <= n <= count:
            if n % 2:
                allowed = allowed_in((n - 1) // 2)
            gateds[n - 1] = softmax_of(n - 1, *raws.pop(n - 1), allowed)
        if n >= 2:
            add_up(n - 2, gateds.pop(n - 2))
    odd_moved = pltpu.roll(acc_odd[...], PADDED - ROPE, 1)
    summed = acc_even[...] + odd_moved + jnp.concatenate([acc_val[...], jnp.zeros((2 * tok, 2 * ROPE), F32)], axis=1)
    whole[...] = summed.astype(BF16).T[:WIDTH]
    core = lax.axis_index("head") % 2
    half = WIDTH // 2
    mine = pl.ds(pl.multiple_of(core * half, 32), half)
    others = pl.ds(pl.multiple_of((1 - core) * half, 32), half)
    early_keep[...] = whole[mine, :tok]
    own_keep[...] = whole[mine, tok:]
    send[...] = whole[others, :]


def query_grads(first_block, d_raw, prior_t, keys_t, gate_rows, after, *refs):
    stage, sems = refs[-2:]
    if first_block == 0:
        out_hbm, done, d_gate = refs[-5:-2]
    else:
        out_hbm, done = refs[-4:-2]
    tok = keys_t.shape[1]
    heads = stage.shape[1] // WIDTH
    size = 2 * TILE // heads
    window = tok + size
    pairs = TILE // size
    even_prior, odd_prior = padded_keys(prior_t[...])
    even_own, odd_own = padded_keys(keys_t[...])
    even = jnp.concatenate([even_prior, even_own], axis=0)
    odd = jnp.concatenate([odd_prior, odd_own], axis=0)
    copies = []
    for at in range(stage.shape[0] // size):
        block = first_block + at
        low, high = block * size, block * size + window
        slopes = [d_raw[pl.ds((2 * block + n) * window, window), :].T for n in range(2)]
        middle = jnp.concatenate([even[low:high, LATENT:], odd[low:high, : 2 * ROPE]], axis=0)
        for column, part in (
            (0, dot_nn(slopes[0], even[low:high, :LATENT])),
            (LATENT, dot_nn(jnp.concatenate(slopes, axis=1), middle)),
            (LATENT + 2 * ROPE, dot_nn(slopes[1], odd[low:high, 2 * ROPE :])),
        ):
            part = part.astype(BF16)
            for p in range(pairs):
                stage[pl.ds(at * size, size), pl.ds(p * PAIR + column, part.shape[1])] = part[
                    p * size : (p + 1) * size
                ]
        copies.append(
            pltpu.make_async_copy(
                stage.at[pl.ds(at * size, size), :], out_hbm.at[pl.ds(low, size), :], sems.at[at]
            )
        )
        copies[-1].start()
    if first_block == 0:
        shape = d_gate.shape
        head = lax.broadcasted_iota(jnp.int32, shape, 0)
        lane = lax.broadcasted_iota(jnp.int32, shape, 1)
        found = jnp.zeros(shape, F32)
        for block in range(tok // size):
            value = jnp.zeros(shape, F32)
            for n in range(2):
                row = gate_rows[pl.ds(2 * block + n, 1), :]
                for part in range(TILE // LANES):
                    held = jnp.broadcast_to(row[:, part * LANES : (part + 1) * LANES], shape)
                    value = jnp.where(head == head_of(shape, n, part, size), held, value)
            shift = size
            while shift < tok:
                value = value + pltpu.roll(value, shift, 1)
                shift *= 2
            found = jnp.where(lane // size == block, value, found)
        d_gate[...] = found
    for copy in copies:
        copy.wait()
    done[...] = jnp.zeros_like(done)


def add_early(keep, other, out):
    out[...] = (keep[...].astype(F32) + other[:, : out.shape[1]].astype(F32)).astype(out.dtype)


def add_own(keep, other, returned, after, out):
    out[...] = (keep[...].astype(F32) + other[:, out.shape[1] :].astype(F32) + returned[...].astype(F32)).astype(out.dtype)


def add_halves(a, b, after, out):
    out[...] = (a[...].astype(F32) + b[...].astype(F32)).astype(out.dtype)


def shifted(value, axis, steps):
    count = lax.axis_size(axis)
    first, last = (max(0, -steps), min(count, count - steps))
    return lax.ppermute(value, axis, [(source, source + steps) for source in range(first, last)])


def shards(queries, latent, gate, d_out, segments):
    tok = latent.shape[0]
    heads = gate.shape[1]
    size = 2 * TILE // heads
    window = tok + size
    blocks = tok // size
    early = max(1, blocks * EARLY // 8)
    half = WIDTH // 2
    columns = heads * tok
    vmem = pl.BlockSpec(memory_space=pltpu.VMEM)
    hbm = pl.BlockSpec(memory_space=pl.ANY)
    params = pltpu.CompilerParams(vmem_limit_bytes=28 * 1024 * 1024)
    kept = pltpu.VMEM
    keys_t = latent.T
    gate_t = gate.T
    ids = segments.reshape(-1, tok)

    def cost(multiply_adds, moved):
        return pl.CostEstimate(flops=2 * multiply_adds, bytes_accessed=moved, transcendentals=0)

    prior_t = shifted(keys_t, "ctx", 1)
    q, g, q_turned, g_turned, keys_t = pl.pallas_call(
        load,
        out_shape=[
            kept(queries.shape, BF16),
            kept(d_out.shape, BF16),
            kept((WIDTH, 2 * early * TILE), BF16),
            kept((LATENT, 2 * early * TILE), BF16),
            kept((WIDTH, tok), BF16),
        ],
        in_specs=[hbm] * 3,
        out_specs=[vmem] * 5,
        scratch_shapes=[pltpu.SemaphoreType.DMA((blocks, 2)), pltpu.SemaphoreType.DMA((1,))],
        compiler_params=params,
        cost_estimate=cost(0, queries.size * 2 + d_out.size * 2),
        name="load",
    )(*[pltpu.with_memory_space_constraint(x, pltpu.HBM) for x in (queries, d_out, keys_t)])
    d_raw, gate_rows, early_keep, own_keep, send = pl.pallas_call(
        grads,
        out_shape=[
            kept((2 * blocks * window, TILE), BF16),
            kept((2 * blocks, TILE), F32),
            kept((half, tok), BF16),
            kept((half, tok), BF16),
            kept((half, 2 * tok), BF16),
        ],
        in_specs=[vmem] * 8,
        out_specs=[vmem] * 5,
        scratch_shapes=[
            pltpu.VMEM((WIDTH, max(1, 2 * (blocks - early)) * TILE), BF16),
            pltpu.VMEM((LATENT, max(1, 2 * (blocks - early)) * TILE), BF16),
            pltpu.VMEM((2 * tok, PADDED), F32),
            pltpu.VMEM((2 * tok, PADDED), F32),
            pltpu.VMEM((2 * tok, LATENT), F32),
            pltpu.VMEM((WIDTH, 2 * tok), BF16),
        ],
        compiler_params=params,
        cost_estimate=cost(2 * columns * window * (WIDTH + LATENT), 0),
        name="grads",
    )(q, g, q_turned, g_turned, prior_t, keys_t, gate_t, ids)
    group = lax.axis_size("head")

    def exchanged(value, step):
        return lax.ppermute(value, "head", [(i, i ^ step) for i in range(group)])

    def small(kernel, name, *operands):
        return pl.pallas_call(
            kernel,
            out_shape=kept((half, tok), BF16),
            in_specs=[vmem] * len(operands),
            out_specs=vmem,
            compiler_params=params,
            name=name,
        )(*operands)

    def query_part(first, count, after, *rest):
        d_gate = [] if rest else [jax.ShapeDtypeStruct((heads, tok), F32)]
        return pl.pallas_call(
            functools.partial(query_grads, first),
            out_shape=[jax.ShapeDtypeStruct(queries.shape, queries.dtype), kept((8, 128), F32)] + d_gate,
            in_specs=[vmem] * 4 + [hbm] * (1 + len(rest)),
            out_specs=[hbm, vmem] + [vmem] * len(d_gate),
            scratch_shapes=[
                pltpu.VMEM((count * size, queries.shape[1]), BF16),
                pltpu.SemaphoreType.DMA((count,)),
            ],
            input_output_aliases={5: 0} if rest else {},
            compiler_params=params,
            cost_estimate=cost(count * 2 * TILE * window * PADDED, count * size * queries.shape[1] * 2),
            name="query_grads",
        )(d_raw, prior_t, keys_t, gate_rows, after, *rest)

    sent = exchanged(send, 1)
    returned = shifted(small(add_early, "add_early", early_keep, sent), "ctx", -1)
    cut = (blocks + 1) // 2
    d_queries, done, d_gate_t = query_part(0, cut, sent)
    total = small(add_own, "add_own", own_keep, sent, returned, done)
    d_queries, done = query_part(cut, blocks - cut, total, d_queries)
    step = 2
    while step < group:
        total = small(add_halves, "add_halves", total, exchanged(total, step), done)
        step *= 2
    other = exchanged(total, 1)
    first = lax.axis_index("head") % 2 == 0
    d_latent_t = jnp.where(first, jnp.concatenate([total, other]), jnp.concatenate([other, total])).astype(F32)
    return d_queries, d_gate_t.T, d_latent_t.T


def solution(mesh):
    placed = (P("ctx", "head"), P("ctx", None), P("ctx", "head"), P("ctx", "head"), P())
    return jax.shard_map(
        shards,
        mesh=mesh,
        in_specs=placed,
        out_specs=(P("ctx", "head"), P("ctx", "head"), P("ctx", None)),
        check_vma=False,
    )
```

```python
import functools

import jax
import jax.numpy as jnp
from jax import lax
from jax.experimental import pallas as pl
from jax.experimental.pallas import tpu as pltpu
from jax.sharding import PartitionSpec as P

LATENT = 512
ROPE = 64
WIDTH = LATENT + ROPE
PAIR = 2 * WIDTH
PADDED = LATENT + 2 * ROPE
SCALE = 192.0 ** (-0.5)
CAP = 20.0
LOG2_E = 1.4426950408889634
LANES = 128
TILE = 256
AHEAD = 8
EARLY = 7
BF16 = jnp.bfloat16
F32 = jnp.float32


def dot_nn(a, b):
    return lax.dot_general(a, b, (((1,), (0,)), ((), ())), preferred_element_type=F32)


def padded_keys(keys_t):
    spare = jnp.zeros((ROPE, keys_t.shape[1]), keys_t.dtype)
    even = jnp.concatenate([keys_t, spare], axis=0).T
    odd = jnp.concatenate([spare, keys_t], axis=0).T
    return even, odd


def latent_grad_t(even, odd, values):
    first = even + jnp.concatenate([values, jnp.zeros((values.shape[0], 2 * ROPE), F32)], axis=1)
    return first.T[:WIDTH] + odd.T[ROPE:]


def query_tile(q, block, odd):
    size = 2 * TILE * WIDTH // q.shape[1]
    rows, at = pl.ds(block * size, size), LATENT if odd else 0
    pairs = TILE // size
    return jnp.concatenate([q[rows, pl.ds(p * PAIR + at, PADDED)] for p in range(pairs)], axis=0)


def cotangent_tile(g, block, odd):
    size = 2 * TILE * LATENT // g.shape[1]
    rows = pl.ds(block * size, size)
    pairs = TILE // size
    return jnp.concatenate([g[rows, pl.ds((2 * p + odd) * LATENT, LATENT)] for p in range(pairs)], axis=0)


def turn(q, g, block, odd, q_turned, g_turned, start):
    cols = pl.ds(start, TILE)
    turned = query_tile(q, block, odd).T
    q_turned[:, cols] = turned[ROPE:] if odd else turned[:WIDTH]
    g_turned[:, cols] = cotangent_tile(g, block, odd).T


def spread(value, block, size):
    lane = lax.broadcasted_iota(jnp.int32, value.shape, 1)
    value = jnp.where(lane // size == block, value, jnp.zeros_like(value))
    shift = size
    while shift < value.shape[1]:
        value = value + pltpu.roll(value, shift, 1)
        shift *= 2
    return value


def head_of(shape, odd, part, size):
    return 2 * (part * (LANES // size) + lax.broadcasted_iota(jnp.int32, shape, 1) // size) + odd


def load(q_hbm, g_hbm, keys_hbm, q, g, q_turned, g_turned, keys_t, sems, key_sem):
    tok, heads = q.shape[0], g.shape[1] // LATENT
    size = 2 * TILE // heads
    blocks, early = tok // size, q_turned.shape[1] // (2 * TILE)
    keys_copy = pltpu.make_async_copy(keys_hbm, keys_t, key_sem.at[0])
    keys_copy.start()

    def copies(block):
        rows = pl.ds(block * size, size)
        return [
            pltpu.make_async_copy(s.at[rows, :], d.at[rows, :], sems.at[block, n])
            for n, (s, d) in enumerate(((q_hbm, q), (g_hbm, g)))
        ]

    for block in range(min(AHEAD, blocks)):
        for copy in copies(block):
            copy.start()
    for block in range(blocks):
        if block + AHEAD < blocks:
            for copy in copies(block + AHEAD):
                copy.start()
        for copy in copies(block):
            copy.wait()
        if block < early:
            for odd in (0, 1):
                turn(q, g, block, odd, q_turned, g_turned, (2 * block + odd) * TILE)
    keys_copy.wait()


def grads(
    q, g, q_turned, g_turned, prior_t, keys_t, gate_t, segments,
    d_raw, gate_rows, early_keep, own_keep, send,
    q_turned_late, g_turned_late, acc_even, acc_odd, acc_val, side_even, side_odd, whole,
):
    tok, heads = gate_t.shape[1], gate_t.shape[0]
    size = 2 * TILE // heads
    window = tok + size
    blocks, early = tok // size, q_turned.shape[1] // (2 * TILE)
    shard = lax.axis_index("ctx")
    keys = jnp.concatenate([prior_t[...].T, keys_t[...].T], axis=0)
    row_own = segments[pl.ds(shard, 1), :]
    row_prior = segments[pl.ds(jnp.maximum(shard - 1, 0), 1), :]
    key_segment = jnp.concatenate(
        [jnp.broadcast_to(row_prior, (tok, tok)).T, jnp.broadcast_to(row_own, (tok, tok)).T], axis=0
    )
    for acc in (acc_even, acc_odd, acc_val, side_even, side_odd):
        acc[...] = jnp.zeros_like(acc)

    def keys_of(block):
        return pl.ds(block * size, window)

    def allowed_in(block):
        key_at = block * size + lax.broadcasted_iota(jnp.int32, (window, tok), 0)
        query_at = block * size + lax.broadcasted_iota(jnp.int32, (window, tok), 1) % size
        query_segment = spread(jnp.broadcast_to(row_own, (8, tok)), block, size)[:1]
        same = key_segment[block * size : block * size + window] == query_segment
        allowed = same & (key_at - tok <= query_at) & ((key_at >= tok) | (shard > 0))
        return allowed

    def gates_of(block, odd):
        spread_gate = spread(gate_t[...], block, size)
        head = lax.broadcasted_iota(jnp.int32, spread_gate.shape, 0)
        return jnp.concatenate(
            [
                jnp.sum(
                    jnp.where(head == head_of(spread_gate.shape, odd, part, size), spread_gate, 0.0),
                    axis=0,
                    keepdims=True,
                )
                for part in range(TILE // LANES)
            ],
            axis=1,
        )

    def scores_of(n):
        block = n // 2
        if block < early:
            q_from, g_from, cols = q_turned, g_turned, pl.ds(n * TILE, TILE)
        else:
            q_from, g_from, cols = q_turned_late, g_turned_late, pl.ds((n - 2 * early) * TILE, TILE)
        held = keys[block * size : block * size + window]
        return dot_nn(held, q_from[:, cols]), dot_nn(held[:, :LATENT], g_from[:, cols])

    def softmax_of(n, raw, d_p, allowed):
        gate = gates_of(n // 2, n % 2)
        gateds = []
        for part in range(TILE // LANES):
            lanes = slice(part * LANES, (part + 1) * LANES)
            squashed = jnp.tanh(raw[:, lanes] * (SCALE / CAP))
            weights = jnp.where(allowed, jnp.exp2((CAP * LOG2_E) * squashed), 0.0)
            opened = jax.nn.sigmoid(gate[:, lanes])
            inverse = 1.0 / jnp.sum(weights, axis=0, keepdims=True)
            mean = jnp.sum(weights * d_p[:, lanes], axis=0, keepdims=True) * inverse
            gate_rows[pl.ds(n, 1), pl.ds(part * LANES, LANES)] = opened * (1.0 - opened) * mean
            gated = weights * (inverse * opened)
            slope = weights * (inverse * opened * SCALE) * (d_p[:, lanes] - mean) * (1.0 - squashed * squashed)
            d_raw[pl.ds(n * window, window), pl.ds(part * LANES, LANES)] = slope.astype(BF16)
            gateds.append(gated.astype(BF16))
        return jnp.concatenate(gateds, axis=1)

    def turned_at(n):
        if n // 2 < early:
            return q_turned, pl.ds(n * TILE, TILE)
        return q_turned_late, pl.ds((n - 2 * early) * TILE, TILE)

    def add_up(n, gated):
        block, odd = n // 2, n % 2
        acc, side = (acc_odd, side_odd) if odd else (acc_even, side_even)
        slope = d_raw[pl.ds(n * window, window), :]
        tile = query_tile(q, block, odd)
        tile = tile[:, PADDED - LATENT :] if odd else tile[:, :LATENT]
        acc[keys_of(block), :] += dot_nn(slope, tile)
        acc_val[keys_of(block), :] += dot_nn(gated, cotangent_tile(g, block, odd))
        above, below = block * size, 2 * tok - window - block * size
        parts = [jnp.zeros((above, TILE), BF16)] * (above > 0) + [slope] + [jnp.zeros((below, TILE), BF16)] * (below > 0)
        all_keys = jnp.concatenate(parts, axis=0).T
        q_from, cols = turned_at(n)
        side[...] += dot_nn(q_from[pl.ds(0 if odd else LATENT, ROPE), cols], all_keys)

    count = 2 * blocks
    raws, gateds = {}, {}
    turned = 2 * early
    for n in range(count + 3):
        while turned < min(count, n + 2):
            turn(q, g, turned // 2, turned % 2, q_turned_late, g_turned_late, (turned - 2 * early) * TILE)
            turned += 1
        if n < count:
            raws[n] = scores_of(n)
        if 1 <= n <= count:
            if n % 2:
                allowed = allowed_in((n - 1) // 2)
            gateds[n - 1] = softmax_of(n - 1, *raws.pop(n - 1), allowed)
        if n >= 3:
            add_up(n - 3, gateds.pop(n - 3))
    even = jnp.concatenate([(acc_even[...] + acc_val[...]).astype(BF16).T.astype(F32), side_even[...]], axis=0)
    odd = jnp.concatenate([side_odd[...], acc_odd[...].astype(BF16).T.astype(F32)], axis=0)
    whole[...] = (even + odd).astype(BF16)
    core = lax.axis_index("head") % 2
    half = WIDTH // 2
    mine = pl.ds(pl.multiple_of(core * half, 32), half)
    others = pl.ds(pl.multiple_of((1 - core) * half, 32), half)
    early_keep[...] = whole[mine, :tok]
    own_keep[...] = whole[mine, tok:]
    send[...] = whole[others, :]


def query_grads(first_block, d_raw, prior_t, keys_t, gate_rows, after, *refs):
    stage, sems = refs[-2:]
    if first_block == 0:
        out_hbm, done, d_gate = refs[-5:-2]
    else:
        out_hbm, done = refs[-4:-2]
    tok = keys_t.shape[1]
    heads = stage.shape[1] // WIDTH
    size = 2 * TILE // heads
    window = tok + size
    pairs = TILE // size
    even_prior, odd_prior = padded_keys(prior_t[...])
    even_own, odd_own = padded_keys(keys_t[...])
    even = jnp.concatenate([even_prior, even_own], axis=0)
    odd = jnp.concatenate([odd_prior, odd_own], axis=0)
    copies = []
    for at in range(stage.shape[0] // size):
        block = first_block + at
        low, high = block * size, block * size + window
        slopes = [d_raw[pl.ds((2 * block + n) * window, window), :].T for n in range(2)]
        middle = jnp.concatenate([even[low:high, LATENT:], odd[low:high, : 2 * ROPE]], axis=0)
        for column, part in (
            (0, dot_nn(slopes[0], even[low:high, :LATENT])),
            (LATENT, dot_nn(jnp.concatenate(slopes, axis=1), middle)),
            (LATENT + 2 * ROPE, dot_nn(slopes[1], odd[low:high, 2 * ROPE :])),
        ):
            part = part.astype(BF16)
            for p in range(pairs):
                stage[pl.ds(at * size, size), pl.ds(p * PAIR + column, part.shape[1])] = part[
                    p * size : (p + 1) * size
                ]
        copies.append(
            pltpu.make_async_copy(
                stage.at[pl.ds(at * size, size), :], out_hbm.at[pl.ds(low, size), :], sems.at[at]
            )
        )
        copies[-1].start()
    if first_block == 0:
        shape = d_gate.shape
        head = lax.broadcasted_iota(jnp.int32, shape, 0)
        lane = lax.broadcasted_iota(jnp.int32, shape, 1)
        found = jnp.zeros(shape, F32)
        for block in range(tok // size):
            value = jnp.zeros(shape, F32)
            for n in range(2):
                row = gate_rows[pl.ds(2 * block + n, 1), :]
                for part in range(TILE // LANES):
                    held = jnp.broadcast_to(row[:, part * LANES : (part + 1) * LANES], shape)
                    value = jnp.where(head == head_of(shape, n, part, size), held, value)
            shift = size
            while shift < tok:
                value = value + pltpu.roll(value, shift, 1)
                shift *= 2
            found = jnp.where(lane // size == block, value, found)
        d_gate[...] = found
    for copy in copies:
        copy.wait()
    done[...] = jnp.zeros_like(done)


def add_early(keep, other, out):
    out[...] = (keep[...].astype(F32) + other[:, : out.shape[1]].astype(F32)).astype(out.dtype)


def add_own(keep, other, returned, after, out):
    out[...] = (keep[...].astype(F32) + other[:, out.shape[1] :].astype(F32) + returned[...].astype(F32)).astype(out.dtype)


def add_halves(a, b, after, out):
    out[...] = (a[...].astype(F32) + b[...].astype(F32)).astype(out.dtype)


def shifted(value, axis, steps):
    count = lax.axis_size(axis)
    first, last = (max(0, -steps), min(count, count - steps))
    return lax.ppermute(value, axis, [(source, source + steps) for source in range(first, last)])


def shards(queries, latent, gate, d_out, segments):
    tok = latent.shape[0]
    heads = gate.shape[1]
    size = 2 * TILE // heads
    window = tok + size
    blocks = tok // size
    early = max(1, blocks * EARLY // 8)
    half = WIDTH // 2
    columns = heads * tok
    vmem = pl.BlockSpec(memory_space=pltpu.VMEM)
    hbm = pl.BlockSpec(memory_space=pl.ANY)
    params = pltpu.CompilerParams(vmem_limit_bytes=28 * 1024 * 1024)
    kept = pltpu.VMEM
    keys_t = latent.T
    gate_t = gate.T
    ids = segments.reshape(-1, tok)

    def cost(multiply_adds, moved):
        return pl.CostEstimate(flops=2 * multiply_adds, bytes_accessed=moved, transcendentals=0)

    prior_t = shifted(keys_t, "ctx", 1)
    q, g, q_turned, g_turned, keys_t = pl.pallas_call(
        load,
        out_shape=[
            kept(queries.shape, BF16),
            kept(d_out.shape, BF16),
            kept((WIDTH, 2 * early * TILE), BF16),
            kept((LATENT, 2 * early * TILE), BF16),
            kept((WIDTH, tok), BF16),
        ],
        in_specs=[hbm] * 3,
        out_specs=[vmem] * 5,
        scratch_shapes=[pltpu.SemaphoreType.DMA((blocks, 2)), pltpu.SemaphoreType.DMA((1,))],
        compiler_params=params,
        cost_estimate=cost(0, queries.size * 2 + d_out.size * 2),
        name="load",
    )(*[pltpu.with_memory_space_constraint(x, pltpu.HBM) for x in (queries, d_out, keys_t)])
    d_raw, gate_rows, early_keep, own_keep, send = pl.pallas_call(
        grads,
        out_shape=[
            kept((2 * blocks * window, TILE), BF16),
            kept((2 * blocks, TILE), F32),
            kept((half, tok), BF16),
            kept((half, tok), BF16),
            kept((half, 2 * tok), BF16),
        ],
        in_specs=[vmem] * 8,
        out_specs=[vmem] * 5,
        scratch_shapes=[
            pltpu.VMEM((WIDTH, max(1, 2 * (blocks - early)) * TILE), BF16),
            pltpu.VMEM((LATENT, max(1, 2 * (blocks - early)) * TILE), BF16),
            pltpu.VMEM((2 * tok, LATENT), F32),
            pltpu.VMEM((2 * tok, LATENT), F32),
            pltpu.VMEM((2 * tok, LATENT), F32),
            pltpu.VMEM((ROPE, 2 * tok), F32),
            pltpu.VMEM((ROPE, 2 * tok), F32),
            pltpu.VMEM((WIDTH, 2 * tok), BF16),
        ],
        compiler_params=params,
        cost_estimate=cost(2 * columns * window * (WIDTH + LATENT), 0),
        name="grads",
    )(q, g, q_turned, g_turned, prior_t, keys_t, gate_t, ids)
    group = lax.axis_size("head")

    def exchanged(value, step):
        return lax.ppermute(value, "head", [(i, i ^ step) for i in range(group)])

    def small(kernel, name, *operands):
        return pl.pallas_call(
            kernel,
            out_shape=kept((half, tok), BF16),
            in_specs=[vmem] * len(operands),
            out_specs=vmem,
            compiler_params=params,
            name=name,
        )(*operands)

    def query_part(first, count, after, *rest):
        d_gate = [] if rest else [jax.ShapeDtypeStruct((heads, tok), F32)]
        return pl.pallas_call(
            functools.partial(query_grads, first),
            out_shape=[jax.ShapeDtypeStruct(queries.shape, queries.dtype), kept((8, 128), F32)] + d_gate,
            in_specs=[vmem] * 4 + [hbm] * (1 + len(rest)),
            out_specs=[hbm, vmem] + [vmem] * len(d_gate),
            scratch_shapes=[
                pltpu.VMEM((count * size, queries.shape[1]), BF16),
                pltpu.SemaphoreType.DMA((count,)),
            ],
            input_output_aliases={5: 0} if rest else {},
            compiler_params=params,
            cost_estimate=cost(count * 2 * TILE * window * PADDED, count * size * queries.shape[1] * 2),
            name="query_grads",
        )(d_raw, prior_t, keys_t, gate_rows, after, *rest)

    sent = exchanged(send, 1)
    returned = shifted(small(add_early, "add_early", early_keep, sent), "ctx", -1)
    cut = (blocks + 1) // 2
    d_queries, done, d_gate_t = query_part(0, cut, sent)
    total = small(add_own, "add_own", own_keep, sent, returned, done)
    d_queries, done = query_part(cut, blocks - cut, total, d_queries)
    step = 2
    while step < group:
        total = small(add_halves, "add_halves", total, exchanged(total, step), done)
        step *= 2
    other = exchanged(total, 1)
    first = lax.axis_index("head") % 2 == 0
    d_latent_t = jnp.where(first, jnp.concatenate([total, other]), jnp.concatenate([other, total])).astype(F32)
    return d_queries, d_gate_t.T, d_latent_t.T


def solution(mesh):
    placed = (P("ctx", "head"), P("ctx", None), P("ctx", "head"), P("ctx", "head"), P())
    return jax.shard_map(
        shards,
        mesh=mesh,
        in_specs=placed,
        out_specs=(P("ctx", "head"), P("ctx", "head"), P("ctx", None)),
        check_vma=False,
    )
```

```python
import functools

import jax
import jax.numpy as jnp
from jax import lax
from jax.experimental import pallas as pl
from jax.experimental.pallas import tpu as pltpu
from jax.sharding import PartitionSpec as P

LATENT = 512
ROPE = 64
WIDTH = LATENT + ROPE
PAIR = 2 * WIDTH
PADDED = LATENT + 2 * ROPE
SCALE = 192.0 ** (-0.5)
CAP = 20.0
LOG2_E = 1.4426950408889634
LANES = 128
TILE = 256
AHEAD = 8
EARLY = 7
BF16 = jnp.bfloat16
F32 = jnp.float32


def dot_nn(a, b):
    return lax.dot_general(a, b, (((1,), (0,)), ((), ())), preferred_element_type=F32)


def padded_keys(keys_t):
    spare = jnp.zeros((ROPE, keys_t.shape[1]), keys_t.dtype)
    even = jnp.concatenate([keys_t, spare], axis=0).T
    odd = jnp.concatenate([spare, keys_t], axis=0).T
    return even, odd


def latent_grad_t(even, odd, values):
    first = even + jnp.concatenate([values, jnp.zeros((values.shape[0], 2 * ROPE), F32)], axis=1)
    return first.T[:WIDTH] + odd.T[ROPE:]


def query_tile(q, block, odd):
    size = 2 * TILE * WIDTH // q.shape[1]
    rows, at = pl.ds(block * size, size), LATENT if odd else 0
    pairs = TILE // size
    return jnp.concatenate([q[rows, pl.ds(p * PAIR + at, PADDED)] for p in range(pairs)], axis=0)


def cotangent_tile(g, block, odd):
    size = 2 * TILE * LATENT // g.shape[1]
    rows = pl.ds(block * size, size)
    pairs = TILE // size
    return jnp.concatenate([g[rows, pl.ds((2 * p + odd) * LATENT, LATENT)] for p in range(pairs)], axis=0)


def turn(q, g, block, odd, q_turned, g_turned, start):
    cols = pl.ds(start, TILE)
    turned = query_tile(q, block, odd).T
    q_turned[:, cols] = turned[ROPE:] if odd else turned[:WIDTH]
    g_turned[:, cols] = cotangent_tile(g, block, odd).T


def spread(value, block, size):
    lane = lax.broadcasted_iota(jnp.int32, value.shape, 1)
    value = jnp.where(lane // size == block, value, jnp.zeros_like(value))
    shift = size
    while shift < value.shape[1]:
        value = value + pltpu.roll(value, shift, 1)
        shift *= 2
    return value


def head_of(shape, odd, part, size):
    return 2 * (part * (LANES // size) + lax.broadcasted_iota(jnp.int32, shape, 1) // size) + odd


def load(q_hbm, g_hbm, keys_hbm, q, g, q_turned, g_turned, keys_t, sems, key_sem):
    tok, heads = q.shape[0], g.shape[1] // LATENT
    size = 2 * TILE // heads
    blocks, early = tok // size, q_turned.shape[1] // (2 * TILE)
    keys_copy = pltpu.make_async_copy(keys_hbm, keys_t, key_sem.at[0])
    keys_copy.start()

    def copies(block):
        rows = pl.ds(block * size, size)
        return [
            pltpu.make_async_copy(s.at[rows, :], d.at[rows, :], sems.at[block, n])
            for n, (s, d) in enumerate(((q_hbm, q), (g_hbm, g)))
        ]

    for block in range(min(AHEAD, blocks)):
        for copy in copies(block):
            copy.start()
    for block in range(blocks):
        if block + AHEAD < blocks:
            for copy in copies(block + AHEAD):
                copy.start()
        for copy in copies(block):
            copy.wait()
        if block < early:
            for odd in (0, 1):
                turn(q, g, block, odd, q_turned, g_turned, (2 * block + odd) * TILE)
    keys_copy.wait()


def grads(
    q, g, q_turned, g_turned, prior_t, keys_t, gate_t, segments,
    d_raw, gate_rows, early_keep, own_keep, send,
    q_turned_late, g_turned_late, acc_even, acc_odd, acc_val, side_even, side_odd, whole,
):
    tok, heads = gate_t.shape[1], gate_t.shape[0]
    size = 2 * TILE // heads
    window = tok + size
    blocks, early = tok // size, q_turned.shape[1] // (2 * TILE)
    shard = lax.axis_index("ctx")
    keys = jnp.concatenate([prior_t[...].T, keys_t[...].T], axis=0)
    row_own = segments[pl.ds(shard, 1), :]
    row_prior = segments[pl.ds(jnp.maximum(shard - 1, 0), 1), :]
    key_segment = jnp.concatenate(
        [jnp.broadcast_to(row_prior, (tok, tok)).T, jnp.broadcast_to(row_own, (tok, tok)).T], axis=0
    )
    for acc in (acc_even, acc_odd, acc_val, side_even, side_odd):
        acc[...] = jnp.zeros_like(acc)

    def keys_of(block):
        return pl.ds(block * size, window)

    def allowed_in(block):
        key_at = block * size + lax.broadcasted_iota(jnp.int32, (window, tok), 0)
        query_at = block * size + lax.broadcasted_iota(jnp.int32, (window, tok), 1) % size
        query_segment = spread(jnp.broadcast_to(row_own, (8, tok)), block, size)[:1]
        same = key_segment[block * size : block * size + window] == query_segment
        allowed = same & (key_at - tok <= query_at) & ((key_at >= tok) | (shard > 0))
        return allowed

    def gates_of(block, odd):
        spread_gate = spread(gate_t[...], block, size)
        head = lax.broadcasted_iota(jnp.int32, spread_gate.shape, 0)
        return jnp.concatenate(
            [
                jnp.sum(
                    jnp.where(head == head_of(spread_gate.shape, odd, part, size), spread_gate, 0.0),
                    axis=0,
                    keepdims=True,
                )
                for part in range(TILE // LANES)
            ],
            axis=1,
        )

    def scores_of(n):
        block = n // 2
        if block < early:
            q_from, g_from, cols = q_turned, g_turned, pl.ds(n * TILE, TILE)
        else:
            q_from, g_from, cols = q_turned_late, g_turned_late, pl.ds((n - 2 * early) * TILE, TILE)
        held = keys[block * size : block * size + window]
        return dot_nn(held, q_from[:, cols]), dot_nn(held[:, :LATENT], g_from[:, cols])

    def softmax_of(n, raw, d_p, allowed):
        gate = gates_of(n // 2, n % 2)
        gateds = []
        for part in range(TILE // LANES):
            lanes = slice(part * LANES, (part + 1) * LANES)
            squashed = jnp.tanh(raw[:, lanes] * (SCALE / CAP))
            weights = jnp.where(allowed, jnp.exp2((CAP * LOG2_E) * squashed), 0.0)
            opened = jax.nn.sigmoid(gate[:, lanes])
            inverse = 1.0 / jnp.sum(weights, axis=0, keepdims=True)
            mean = jnp.sum(weights * d_p[:, lanes], axis=0, keepdims=True) * inverse
            gate_rows[pl.ds(n, 1), pl.ds(part * LANES, LANES)] = opened * (1.0 - opened) * mean
            gated = weights * (inverse * opened)
            slope = weights * (inverse * opened * SCALE) * (d_p[:, lanes] - mean) * (1.0 - squashed * squashed)
            d_raw[pl.ds(n * window, window), pl.ds(part * LANES, LANES)] = slope.astype(BF16)
            gateds.append(gated.astype(BF16))
        return jnp.concatenate(gateds, axis=1)

    def turned_at(n):
        if n // 2 < early:
            return q_turned, pl.ds(n * TILE, TILE)
        return q_turned_late, pl.ds((n - 2 * early) * TILE, TILE)

    def add_up(n, gated):
        block, odd = n // 2, n % 2
        acc, side = (acc_odd, side_odd) if odd else (acc_even, side_even)
        slope = d_raw[pl.ds(n * window, window), :]
        tile = query_tile(q, block, odd)
        tile = tile[:, PADDED - LATENT :] if odd else tile[:, :LATENT]
        acc[keys_of(block), :] += dot_nn(slope, tile)
        acc_val[keys_of(block), :] += dot_nn(gated, cotangent_tile(g, block, odd))
        above, below = block * size, 2 * tok - window - block * size
        parts = [jnp.zeros((above, TILE), BF16)] * (above > 0) + [slope] + [jnp.zeros((below, TILE), BF16)] * (below > 0)
        all_keys = jnp.concatenate(parts, axis=0).T
        q_from, cols = turned_at(n)
        side[...] += dot_nn(q_from[pl.ds(0 if odd else LATENT, ROPE), cols], all_keys)

    count = 2 * blocks
    raws, gateds = {}, {}
    turned = 2 * early
    for n in range(count + 3):
        while turned < min(count, n + 2):
            turn(q, g, turned // 2, turned % 2, q_turned_late, g_turned_late, (turned - 2 * early) * TILE)
            turned += 1
        if n < count:
            raws[n] = scores_of(n)
        if 1 <= n <= count:
            if n % 2:
                allowed = allowed_in((n - 1) // 2)
            gateds[n - 1] = softmax_of(n - 1, *raws.pop(n - 1), allowed)
        if n >= 3:
            add_up(n - 3, gateds.pop(n - 3))
    even = jnp.concatenate([(acc_even[...] + acc_val[...]).astype(BF16).T.astype(F32), side_even[...]], axis=0)
    odd = jnp.concatenate([side_odd[...], acc_odd[...].astype(BF16).T.astype(F32)], axis=0)
    whole[...] = (even + odd).astype(BF16)
    core = lax.axis_index("head") % 2
    half = WIDTH // 2
    mine = pl.ds(pl.multiple_of(core * half, 32), half)
    others = pl.ds(pl.multiple_of((1 - core) * half, 32), half)
    early_keep[...] = whole[others, :tok]
    own_keep[...] = whole[mine, tok:]
    send[:, :tok] = whole[mine, :tok]
    send[:, tok:] = whole[others, tok:]


def query_grads(first_block, d_raw, prior_t, keys_t, gate_rows, after, *refs):
    stage, sems = refs[-2:]
    if first_block == 0:
        out_hbm, done, d_gate = refs[-5:-2]
    else:
        out_hbm, done = refs[-4:-2]
    tok = keys_t.shape[1]
    heads = stage.shape[1] // WIDTH
    size = 2 * TILE // heads
    window = tok + size
    pairs = TILE // size
    even_prior, odd_prior = padded_keys(prior_t[...])
    even_own, odd_own = padded_keys(keys_t[...])
    even = jnp.concatenate([even_prior, even_own], axis=0)
    odd = jnp.concatenate([odd_prior, odd_own], axis=0)
    copies = []
    for at in range(stage.shape[0] // size):
        block = first_block + at
        low, high = block * size, block * size + window
        slopes = [d_raw[pl.ds((2 * block + n) * window, window), :].T for n in range(2)]
        middle = jnp.concatenate([even[low:high, LATENT:], odd[low:high, : 2 * ROPE]], axis=0)
        for column, part in (
            (0, dot_nn(slopes[0], even[low:high, :LATENT])),
            (LATENT, dot_nn(jnp.concatenate(slopes, axis=1), middle)),
            (LATENT + 2 * ROPE, dot_nn(slopes[1], odd[low:high, 2 * ROPE :])),
        ):
            part = part.astype(BF16)
            for p in range(pairs):
                stage[pl.ds(at * size, size), pl.ds(p * PAIR + column, part.shape[1])] = part[
                    p * size : (p + 1) * size
                ]
        copies.append(
            pltpu.make_async_copy(
                stage.at[pl.ds(at * size, size), :], out_hbm.at[pl.ds(low, size), :], sems.at[at]
            )
        )
        copies[-1].start()
    if first_block == 0:
        shape = d_gate.shape
        head = lax.broadcasted_iota(jnp.int32, shape, 0)
        lane = lax.broadcasted_iota(jnp.int32, shape, 1)
        found = jnp.zeros(shape, F32)
        for block in range(tok // size):
            value = jnp.zeros(shape, F32)
            for n in range(2):
                row = gate_rows[pl.ds(2 * block + n, 1), :]
                for part in range(TILE // LANES):
                    held = jnp.broadcast_to(row[:, part * LANES : (part + 1) * LANES], shape)
                    value = jnp.where(head == head_of(shape, n, part, size), held, value)
            shift = size
            while shift < tok:
                value = value + pltpu.roll(value, shift, 1)
                shift *= 2
            found = jnp.where(lane // size == block, value, found)
        d_gate[...] = found
    for copy in copies:
        copy.wait()
    done[...] = jnp.zeros_like(done)


def add_early(keep, other, out):
    out[...] = (keep[...].astype(F32) + other[:, : out.shape[1]].astype(F32)).astype(out.dtype)


def add_own(keep, other, returned, after, out):
    out[...] = (keep[...].astype(F32) + other[:, out.shape[1] :].astype(F32) + returned[...].astype(F32)).astype(out.dtype)


def add_halves(a, b, after, out):
    out[...] = (a[...].astype(F32) + b[...].astype(F32)).astype(out.dtype)


def shards(queries, latent, gate, d_out, segments):
    tok = latent.shape[0]
    heads = gate.shape[1]
    size = 2 * TILE // heads
    window = tok + size
    blocks = tok // size
    early = max(1, blocks * EARLY // 8)
    half = WIDTH // 2
    columns = heads * tok
    vmem = pl.BlockSpec(memory_space=pltpu.VMEM)
    hbm = pl.BlockSpec(memory_space=pl.ANY)
    params = pltpu.CompilerParams(vmem_limit_bytes=28 * 1024 * 1024)
    kept = pltpu.VMEM
    keys_t = latent.T
    gate_t = gate.T
    ids = segments.reshape(-1, tok)

    def cost(multiply_adds, moved):
        return pl.CostEstimate(flops=2 * multiply_adds, bytes_accessed=moved, transcendentals=0)

    group, shards_of = lax.axis_size("head"), lax.axis_size("ctx")

    def to_shard(value, steps, cross):
        pairs = [
            (i * group + h, (i + steps) * group + (h ^ cross))
            for i in range(shards_of)
            if 0 <= i + steps < shards_of
            for h in range(group)
        ]
        return lax.ppermute(value, ("ctx", "head"), pairs)

    prior_t = to_shard(keys_t, 1, 0)
    q, g, q_turned, g_turned, keys_t = pl.pallas_call(
        load,
        out_shape=[
            kept(queries.shape, BF16),
            kept(d_out.shape, BF16),
            kept((WIDTH, 2 * early * TILE), BF16),
            kept((LATENT, 2 * early * TILE), BF16),
            kept((WIDTH, tok), BF16),
        ],
        in_specs=[hbm] * 3,
        out_specs=[vmem] * 5,
        scratch_shapes=[pltpu.SemaphoreType.DMA((blocks, 2)), pltpu.SemaphoreType.DMA((1,))],
        compiler_params=params,
        cost_estimate=cost(0, queries.size * 2 + d_out.size * 2),
        name="load",
    )(*[pltpu.with_memory_space_constraint(x, pltpu.HBM) for x in (queries, d_out, keys_t)])
    d_raw, gate_rows, early_keep, own_keep, send = pl.pallas_call(
        grads,
        out_shape=[
            kept((2 * blocks * window, TILE), BF16),
            kept((2 * blocks, TILE), F32),
            kept((half, tok), BF16),
            kept((half, tok), BF16),
            kept((half, 2 * tok), BF16),
        ],
        in_specs=[vmem] * 8,
        out_specs=[vmem] * 5,
        scratch_shapes=[
            pltpu.VMEM((WIDTH, max(1, 2 * (blocks - early)) * TILE), BF16),
            pltpu.VMEM((LATENT, max(1, 2 * (blocks - early)) * TILE), BF16),
            pltpu.VMEM((2 * tok, LATENT), F32),
            pltpu.VMEM((2 * tok, LATENT), F32),
            pltpu.VMEM((2 * tok, LATENT), F32),
            pltpu.VMEM((ROPE, 2 * tok), F32),
            pltpu.VMEM((ROPE, 2 * tok), F32),
            pltpu.VMEM((WIDTH, 2 * tok), BF16),
        ],
        compiler_params=params,
        cost_estimate=cost(2 * columns * window * (WIDTH + LATENT), 0),
        name="grads",
    )(q, g, q_turned, g_turned, prior_t, keys_t, gate_t, ids)
    def exchanged(value, step):
        return lax.ppermute(value, "head", [(i, i ^ step) for i in range(group)])

    def small(kernel, name, *operands):
        return pl.pallas_call(
            kernel,
            out_shape=kept((half, tok), BF16),
            in_specs=[vmem] * len(operands),
            out_specs=vmem,
            compiler_params=params,
            name=name,
        )(*operands)

    def query_part(first, count, after, *rest):
        d_gate = [] if rest else [jax.ShapeDtypeStruct((heads, tok), F32)]
        return pl.pallas_call(
            functools.partial(query_grads, first),
            out_shape=[jax.ShapeDtypeStruct(queries.shape, queries.dtype), kept((8, 128), F32)] + d_gate,
            in_specs=[vmem] * 4 + [hbm] * (1 + len(rest)),
            out_specs=[hbm, vmem] + [vmem] * len(d_gate),
            scratch_shapes=[
                pltpu.VMEM((count * size, queries.shape[1]), BF16),
                pltpu.SemaphoreType.DMA((count,)),
            ],
            input_output_aliases={5: 0} if rest else {},
            compiler_params=params,
            cost_estimate=cost(count * 2 * TILE * window * PADDED, count * size * queries.shape[1] * 2),
            name="query_grads",
        )(d_raw, prior_t, keys_t, gate_rows, after, *rest)

    sent = exchanged(send, 1)
    returned = to_shard(small(add_early, "add_early", early_keep, sent), -1, 1)
    cut = (blocks + 1) // 2
    d_queries, done, d_gate_t = query_part(0, cut, sent)
    total = small(add_own, "add_own", own_keep, sent, returned, done)
    d_queries, done = query_part(cut, blocks - cut, total, d_queries)
    step = 2
    while step < group:
        total = small(add_halves, "add_halves", total, exchanged(total, step), done)
        step *= 2
    other = exchanged(total, 1)
    first = lax.axis_index("head") % 2 == 0
    d_latent_t = jnp.where(first, jnp.concatenate([total, other]), jnp.concatenate([other, total])).astype(F32)
    return d_queries, d_gate_t.T, d_latent_t.T


def solution(mesh):
    placed = (P("ctx", "head"), P("ctx", None), P("ctx", "head"), P("ctx", "head"), P())
    return jax.shard_map(
        shards,
        mesh=mesh,
        in_specs=placed,
        out_specs=(P("ctx", "head"), P("ctx", "head"), P("ctx", None)),
        check_vma=False,
    )
```

```python
import functools

import jax
import jax.numpy as jnp
from jax import lax
from jax.experimental import pallas as pl
from jax.experimental.pallas import tpu as pltpu
from jax.sharding import PartitionSpec as P

LATENT = 512
ROPE = 64
WIDTH = LATENT + ROPE
PAIR = 2 * WIDTH
PADDED = LATENT + 2 * ROPE
SCALE = 192.0 ** (-0.5)
CAP = 20.0
LOG2_E = 1.4426950408889634
LANES = 128
TILE = 256
AHEAD = 8
EARLY = 7
BF16 = jnp.bfloat16
F32 = jnp.float32


def dot_nn(a, b):
    return lax.dot_general(a, b, (((1,), (0,)), ((), ())), preferred_element_type=F32)


def padded_keys(keys_t):
    spare = jnp.zeros((ROPE, keys_t.shape[1]), keys_t.dtype)
    even = jnp.concatenate([keys_t, spare], axis=0).T
    odd = jnp.concatenate([spare, keys_t], axis=0).T
    return even, odd


def latent_grad_t(even, odd, values):
    first = even + jnp.concatenate([values, jnp.zeros((values.shape[0], 2 * ROPE), F32)], axis=1)
    return first.T[:WIDTH] + odd.T[ROPE:]


def query_tile(q, block, odd):
    size = 2 * TILE * WIDTH // q.shape[1]
    rows, at = pl.ds(block * size, size), LATENT if odd else 0
    pairs = TILE // size
    return jnp.concatenate([q[rows, pl.ds(p * PAIR + at, PADDED)] for p in range(pairs)], axis=0)


def cotangent_tile(g, block, odd):
    size = 2 * TILE * LATENT // g.shape[1]
    rows = pl.ds(block * size, size)
    pairs = TILE // size
    return jnp.concatenate([g[rows, pl.ds((2 * p + odd) * LATENT, LATENT)] for p in range(pairs)], axis=0)


def turn(q, g, block, odd, q_turned, g_turned, start):
    cols = pl.ds(start, TILE)
    turned = query_tile(q, block, odd).T
    q_turned[:, cols] = turned[ROPE:] if odd else turned[:WIDTH]
    g_turned[:, cols] = cotangent_tile(g, block, odd).T


def spread(value, block, size):
    lane = lax.broadcasted_iota(jnp.int32, value.shape, 1)
    value = jnp.where(lane // size == block, value, jnp.zeros_like(value))
    shift = size
    while shift < value.shape[1]:
        value = value + pltpu.roll(value, shift, 1)
        shift *= 2
    return value


def head_of(shape, odd, part, size):
    return 2 * (part * (LANES // size) + lax.broadcasted_iota(jnp.int32, shape, 1) // size) + odd


def load(q_hbm, g_hbm, keys_hbm, q, g, q_turned, g_turned, keys_t, sems, key_sem):
    tok, heads = q.shape[0], g.shape[1] // LATENT
    size = 2 * TILE // heads
    blocks, early = tok // size, q_turned.shape[1] // (2 * TILE)
    keys_copy = pltpu.make_async_copy(keys_hbm, keys_t, key_sem.at[0])
    keys_copy.start()

    def copies(block):
        rows = pl.ds(block * size, size)
        return [
            pltpu.make_async_copy(s.at[rows, :], d.at[rows, :], sems.at[block, n])
            for n, (s, d) in enumerate(((q_hbm, q), (g_hbm, g)))
        ]

    for block in range(min(AHEAD, blocks)):
        for copy in copies(block):
            copy.start()
    for block in range(blocks):
        if block + AHEAD < blocks:
            for copy in copies(block + AHEAD):
                copy.start()
        for copy in copies(block):
            copy.wait()
        if block < early:
            for odd in (0, 1):
                turn(q, g, block, odd, q_turned, g_turned, (2 * block + odd) * TILE)
    keys_copy.wait()


def grads(
    q, g, q_turned, g_turned, prior_t, keys_t, gate_t, segments,
    d_raw, gate_rows, early_keep, own_keep, send,
    q_turned_late, g_turned_late, acc_even, acc_odd, acc_val, side_even, side_odd, whole,
):
    tok, heads = gate_t.shape[1], gate_t.shape[0]
    size = 2 * TILE // heads
    window = tok + size
    blocks, early = tok // size, q_turned.shape[1] // (2 * TILE)
    shard = lax.axis_index("ctx")
    keys = jnp.concatenate([prior_t[...].T, keys_t[...].T], axis=0)
    row_own = segments[pl.ds(shard, 1), :]
    row_prior = segments[pl.ds(jnp.maximum(shard - 1, 0), 1), :]
    key_segment = jnp.concatenate(
        [jnp.broadcast_to(row_prior, (tok, tok)).T, jnp.broadcast_to(row_own, (tok, tok)).T], axis=0
    )
    for acc in (acc_even, acc_odd, acc_val, side_even, side_odd):
        acc[...] = jnp.zeros_like(acc)

    def keys_of(block):
        return pl.ds(block * size, window)

    def allowed_in(block):
        key_at = block * size + lax.broadcasted_iota(jnp.int32, (window, tok), 0)
        query_at = block * size + lax.broadcasted_iota(jnp.int32, (window, tok), 1) % size
        query_segment = spread(jnp.broadcast_to(row_own, (8, tok)), block, size)[:1]
        same = key_segment[block * size : block * size + window] == query_segment
        allowed = same & (key_at - tok <= query_at) & ((key_at >= tok) | (shard > 0))
        return allowed

    def gates_of(block, odd):
        spread_gate = spread(gate_t[...], block, size)
        head = lax.broadcasted_iota(jnp.int32, spread_gate.shape, 0)
        return jnp.concatenate(
            [
                jnp.sum(
                    jnp.where(head == head_of(spread_gate.shape, odd, part, size), spread_gate, 0.0),
                    axis=0,
                    keepdims=True,
                )
                for part in range(TILE // LANES)
            ],
            axis=1,
        )

    def scores_of(n):
        block = n // 2
        if block < early:
            q_from, g_from, cols = q_turned, g_turned, pl.ds(n * TILE, TILE)
        else:
            q_from, g_from, cols = q_turned_late, g_turned_late, pl.ds((n - 2 * early) * TILE, TILE)
        held = keys[block * size : block * size + window]
        return dot_nn(held, q_from[:, cols]), dot_nn(held[:, :LATENT], g_from[:, cols])

    def softmax_of(n, raw, d_p, allowed):
        gate = gates_of(n // 2, n % 2)
        gateds = []
        for part in range(TILE // LANES):
            lanes = slice(part * LANES, (part + 1) * LANES)
            squashed = jnp.tanh(raw[:, lanes] * (SCALE / CAP))
            weights = jnp.where(allowed, jnp.exp2((CAP * LOG2_E) * squashed), 0.0)
            opened = jax.nn.sigmoid(gate[:, lanes])
            inverse = 1.0 / jnp.sum(weights, axis=0, keepdims=True)
            mean = jnp.sum(weights * d_p[:, lanes], axis=0, keepdims=True) * inverse
            gate_rows[pl.ds(n, 1), pl.ds(part * LANES, LANES)] = opened * (1.0 - opened) * mean
            gated = weights * (inverse * opened)
            slope = weights * (inverse * opened * SCALE) * (d_p[:, lanes] - mean) * (1.0 - squashed * squashed)
            d_raw[pl.ds(n * window, window), pl.ds(part * LANES, LANES)] = slope.astype(BF16)
            gateds.append(gated.astype(BF16))
        return jnp.concatenate(gateds, axis=1)

    def turned_at(n):
        if n // 2 < early:
            return q_turned, pl.ds(n * TILE, TILE)
        return q_turned_late, pl.ds((n - 2 * early) * TILE, TILE)

    def add_up(n, gated):
        block, odd = n // 2, n % 2
        acc, side = (acc_odd, side_odd) if odd else (acc_even, side_even)
        slope = d_raw[pl.ds(n * window, window), :]
        tile = query_tile(q, block, odd)
        tile = tile[:, PADDED - LATENT :] if odd else tile[:, :LATENT]
        acc[keys_of(block), :] += dot_nn(slope, tile)
        acc_val[keys_of(block), :] += dot_nn(gated, cotangent_tile(g, block, odd))
        above, below = block * size, 2 * tok - window - block * size
        parts = [jnp.zeros((above, TILE), BF16)] * (above > 0) + [slope] + [jnp.zeros((below, TILE), BF16)] * (below > 0)
        all_keys = jnp.concatenate(parts, axis=0).T
        q_from, cols = turned_at(n)
        side[...] += dot_nn(q_from[pl.ds(0 if odd else LATENT, ROPE), cols], all_keys)

    count = 2 * blocks
    raws, gateds = {}, {}
    turned = 2 * early
    for n in range(count + 3):
        while turned < min(count, n + 2):
            turn(q, g, turned // 2, turned % 2, q_turned_late, g_turned_late, (turned - 2 * early) * TILE)
            turned += 1
        if n < count:
            raws[n] = scores_of(n)
        if 1 <= n <= count:
            if n % 2:
                allowed = allowed_in((n - 1) // 2)
            gateds[n - 1] = softmax_of(n - 1, *raws.pop(n - 1), allowed)
        if n >= 3:
            add_up(n - 3, gateds.pop(n - 3))
    even = jnp.concatenate([(acc_even[...] + acc_val[...]).astype(BF16).T.astype(F32), side_even[...]], axis=0)
    odd = jnp.concatenate([side_odd[...], acc_odd[...].astype(BF16).T.astype(F32)], axis=0)
    whole[...] = (even + odd).astype(BF16)
    core = lax.axis_index("head") % 2
    half = WIDTH // 2
    mine = pl.ds(pl.multiple_of(core * half, 32), half)
    others = pl.ds(pl.multiple_of((1 - core) * half, 32), half)
    early_keep[...] = whole[others, :tok]
    own_keep[...] = whole[mine, tok:]
    send[:, :tok] = whole[mine, :tok]
    send[:, tok:] = whole[others, tok:]


def query_grads(first_block, d_raw, prior_t, keys_t, gate_rows, after, *refs):
    stage, sems = refs[-2:]
    if first_block == 0:
        out_hbm, done, d_gate = refs[-5:-2]
    else:
        out_hbm, done = refs[-4:-2]
    tok = keys_t.shape[1]
    heads = stage.shape[1] // WIDTH
    size = 2 * TILE // heads
    window = tok + size
    pairs = TILE // size
    even_prior, odd_prior = padded_keys(prior_t[...])
    even_own, odd_own = padded_keys(keys_t[...])
    even = jnp.concatenate([even_prior, even_own], axis=0)
    odd = jnp.concatenate([odd_prior, odd_own], axis=0)
    copies = []
    for at in range(stage.shape[0] // size):
        block = first_block + at
        low, high = block * size, block * size + window
        slopes = [d_raw[pl.ds((2 * block + n) * window, window), :].T for n in range(2)]
        middle = jnp.concatenate([even[low:high, LATENT:], odd[low:high, : 2 * ROPE]], axis=0)
        for column, part in (
            (0, dot_nn(slopes[0], even[low:high, :LATENT])),
            (LATENT, dot_nn(jnp.concatenate(slopes, axis=1), middle)),
            (LATENT + 2 * ROPE, dot_nn(slopes[1], odd[low:high, 2 * ROPE :])),
        ):
            part = part.astype(BF16)
            for p in range(pairs):
                stage[pl.ds(at * size, size), pl.ds(p * PAIR + column, part.shape[1])] = part[
                    p * size : (p + 1) * size
                ]
        copies.append(
            pltpu.make_async_copy(
                stage.at[pl.ds(at * size, size), :], out_hbm.at[pl.ds(low, size), :], sems.at[at]
            )
        )
        copies[-1].start()
    if first_block == 0:
        shape = d_gate.shape
        head = lax.broadcasted_iota(jnp.int32, shape, 0)
        lane = lax.broadcasted_iota(jnp.int32, shape, 1)
        found = jnp.zeros(shape, F32)
        for block in range(tok // size):
            value = jnp.zeros(shape, F32)
            for n in range(2):
                row = gate_rows[pl.ds(2 * block + n, 1), :]
                for part in range(TILE // LANES):
                    held = jnp.broadcast_to(row[:, part * LANES : (part + 1) * LANES], shape)
                    value = jnp.where(head == head_of(shape, n, part, size), held, value)
            shift = size
            while shift < tok:
                value = value + pltpu.roll(value, shift, 1)
                shift *= 2
            found = jnp.where(lane // size == block, value, found)
        d_gate[...] = found
    for copy in copies:
        copy.wait()
    done[...] = jnp.zeros_like(done)


def add_early(keep, other, out):
    out[...] = (keep[...].astype(F32) + other[:, : out.shape[1]].astype(F32)).astype(out.dtype)


def add_own(keep, other, returned, after, out):
    out[...] = (keep[...].astype(F32) + other[:, out.shape[1] :].astype(F32) + returned[...].astype(F32)).astype(out.dtype)


def join(a, b, after, out):
    out[pl.ds(0, a.shape[0]), :] = a[...]
    out[pl.ds(a.shape[0], a.shape[0]), :] = b[...]


def add_halves(a, b, after, out):
    out[...] = (a[...].astype(F32) + b[...].astype(F32)).astype(out.dtype)


def shards(queries, latent, gate, d_out, segments):
    tok = latent.shape[0]
    heads = gate.shape[1]
    size = 2 * TILE // heads
    window = tok + size
    blocks = tok // size
    early = max(1, blocks * EARLY // 8)
    half = WIDTH // 2
    columns = heads * tok
    vmem = pl.BlockSpec(memory_space=pltpu.VMEM)
    hbm = pl.BlockSpec(memory_space=pl.ANY)
    params = pltpu.CompilerParams(vmem_limit_bytes=28 * 1024 * 1024)
    kept = pltpu.VMEM
    keys_t = latent.T
    gate_t = gate.T
    ids = segments.reshape(-1, tok)

    def cost(multiply_adds, moved):
        return pl.CostEstimate(flops=2 * multiply_adds, bytes_accessed=moved, transcendentals=0)

    group, shards_of = lax.axis_size("head"), lax.axis_size("ctx")

    def to_shard(value, steps, cross):
        pairs = [
            (i * group + h, (i + steps) * group + (h ^ cross))
            for i in range(shards_of)
            if 0 <= i + steps < shards_of
            for h in range(group)
        ]
        return lax.ppermute(value, ("ctx", "head"), pairs)

    prior_t = to_shard(keys_t, 1, 0)
    q, g, q_turned, g_turned, keys_t = pl.pallas_call(
        load,
        out_shape=[
            kept(queries.shape, BF16),
            kept(d_out.shape, BF16),
            kept((WIDTH, 2 * early * TILE), BF16),
            kept((LATENT, 2 * early * TILE), BF16),
            kept((WIDTH, tok), BF16),
        ],
        in_specs=[hbm] * 3,
        out_specs=[vmem] * 5,
        scratch_shapes=[pltpu.SemaphoreType.DMA((blocks, 2)), pltpu.SemaphoreType.DMA((1,))],
        compiler_params=params,
        cost_estimate=cost(0, queries.size * 2 + d_out.size * 2),
        name="load",
    )(*[pltpu.with_memory_space_constraint(x, pltpu.HBM) for x in (queries, d_out, keys_t)])
    d_raw, gate_rows, early_keep, own_keep, send = pl.pallas_call(
        grads,
        out_shape=[
            kept((2 * blocks * window, TILE), BF16),
            kept((2 * blocks, TILE), F32),
            kept((half, tok), BF16),
            kept((half, tok), BF16),
            kept((half, 2 * tok), BF16),
        ],
        in_specs=[vmem] * 8,
        out_specs=[vmem] * 5,
        scratch_shapes=[
            pltpu.VMEM((WIDTH, max(1, 2 * (blocks - early)) * TILE), BF16),
            pltpu.VMEM((LATENT, max(1, 2 * (blocks - early)) * TILE), BF16),
            pltpu.VMEM((2 * tok, LATENT), F32),
            pltpu.VMEM((2 * tok, LATENT), F32),
            pltpu.VMEM((2 * tok, LATENT), F32),
            pltpu.VMEM((ROPE, 2 * tok), F32),
            pltpu.VMEM((ROPE, 2 * tok), F32),
            pltpu.VMEM((WIDTH, 2 * tok), BF16),
        ],
        compiler_params=params,
        cost_estimate=cost(2 * columns * window * (WIDTH + LATENT), 0),
        name="grads",
    )(q, g, q_turned, g_turned, prior_t, keys_t, gate_t, ids)
    def exchanged(value, step):
        return lax.ppermute(value, "head", [(i, i ^ step) for i in range(group)])

    def small(kernel, name, *operands):
        return pl.pallas_call(
            kernel,
            out_shape=kept((half, tok), BF16),
            in_specs=[vmem] * len(operands),
            out_specs=vmem,
            compiler_params=params,
            name=name,
        )(*operands)

    def query_part(first, count, after, *rest):
        d_gate = [] if rest else [jax.ShapeDtypeStruct((heads, tok), F32)]
        return pl.pallas_call(
            functools.partial(query_grads, first),
            out_shape=[jax.ShapeDtypeStruct(queries.shape, queries.dtype), kept((8, 128), F32)] + d_gate,
            in_specs=[vmem] * 4 + [hbm] * (1 + len(rest)),
            out_specs=[hbm, vmem] + [vmem] * len(d_gate),
            scratch_shapes=[
                pltpu.VMEM((count * size, queries.shape[1]), BF16),
                pltpu.SemaphoreType.DMA((count,)),
            ],
            input_output_aliases={5: 0} if rest else {},
            compiler_params=params,
            cost_estimate=cost(count * 2 * TILE * window * PADDED, count * size * queries.shape[1] * 2),
            name="query_grads",
        )(d_raw, prior_t, keys_t, gate_rows, after, *rest)

    sent = exchanged(send, 1)
    returned = to_shard(small(add_early, "add_early", early_keep, sent), -1, 1)
    cut = (blocks + 1) // 2
    d_queries, done, d_gate_t = query_part(0, cut, sent)
    total = small(add_own, "add_own", own_keep, sent, returned, done)
    d_queries, done = query_part(cut, blocks - cut, total, d_queries)
    step = 2
    while 2 * step < group:
        total = small(add_halves, "add_halves", total, exchanged(total, step), done)
        step *= 2
    both = pl.pallas_call(
        join,
        out_shape=kept((2 * half, tok), BF16),
        in_specs=[vmem, vmem, hbm],
        out_specs=vmem,
        compiler_params=params,
        name="join",
    )(total, exchanged(total, step ^ 1), done)
    given = exchanged(both, 1)
    own_half = both[:half].astype(F32) + given[half:].astype(F32)
    other_half = both[half:].astype(F32) + given[:half].astype(F32)
    first = lax.axis_index("head") % 2 == 0
    d_latent_t = jnp.where(
        first, jnp.concatenate([own_half, other_half]), jnp.concatenate([other_half, own_half])
    )
    return d_queries, d_gate_t.T, d_latent_t.T


def solution(mesh):
    placed = (P("ctx", "head"), P("ctx", None), P("ctx", "head"), P("ctx", "head"), P())
    return jax.shard_map(
        shards,
        mesh=mesh,
        in_specs=placed,
        out_specs=(P("ctx", "head"), P("ctx", "head"), P("ctx", None)),
        check_vma=False,
    )
```
